512 devices in a mesh: tract: 8 (over y, core), visit: 64 (over x, z).
Axes of the slice: x: 4, y: 4, z: 16, core: 2. Of those that a mesh axis runs over, the one named last changes fastest.
Arguments:
- images: bfloat16 [8, 2048, 6400], P('tract', 'visit'), may hold values from -6 to 6
- coefficients: bfloat16 [8, 2048, 96], P('tract', 'visit'), may hold values from -3 to 3
- orders: int32 [8, 2048], P('tract', 'visit'), may hold values from 0 to 2
- resample: bfloat16 [8, 2048, 3200], P('tract', 'visit'), may hold values from -1 to 1
- weights: bfloat16 [8, 2048], P('tract', 'visit'), may hold values from 0.049804688 to 0.5
- routes: int32 [8, 2048, 2], P('tract', 'visit'), may hold values from 0 to 63, all different within a row; in each aligned block of 32 rows (0 to 31, 32 to 63, ..., all dimensions but the last counted through in order) at most 2 rows name the same one
- offsets: int32 [8, 2048, 2, 2], P('tract', 'visit'), may hold values from 0 to 216
Outputs:
- coadd_flux: float32 [64, 256, 256], P('visit', 'tract')
- coadd_weight: float32 [64, 256, 256], P('visit', 'tract')
The draws below stay inside these ranges and needn't reach their ends.
Inputs may be any that keep to these rules, and one draw needn't show every extreme that they name: `routes`: in the rows of one device (32 blocks, aligned), no patch is named by more than 2 pairs of block and margin; the 2 patches of a block differ.
All inputs are finite; a program needn't handle non-finite values.
Results may differ from the reference program's by a relative error of at most 0.0065.
Values may be sent and summed in bfloat16 or wider, within the bound.
No kernel may reach another device: no remote copies, remote signals or barrier semaphores. Data moves between devices by JAX's collectives and lax.ppermute only.
A program may use at most 64 MiB of HBM per device.

```python
import math
import jax
import jax.numpy as jnp
import numpy as np
from jax import lax

KSIZE = 41
NBASIS = 16
NTERMS = 6
TOP = 2
BLK = 40
B_DEV = 32
PATCH = 256
HALF = 20
BLKIN = 80
NB = 2048
CAP = 2
N_TRACT = 8
N_VISIT = 64


def draw_resample(key, part):
    key = jax.random.fold_in(key, 7)
    key_diag, key_off = jax.random.split(key, 2)
    lead = (N_TRACT, NB, 2, BLK, 1)
    full = (N_TRACT, NB, 2, BLK, BLK)
    spread = float(BLK) ** (-0.5)
    diagonal = jax.random.uniform(key_diag, lead, jnp.float32, 0.6, 1.0)
    off_diag = jax.random.uniform(key_off, full, jnp.float32, -1.0, 1.0) * (0.69 * spread)
    row_ids = jnp.arange(BLK, dtype=jnp.int32)[:, None]
    col_ids = jnp.arange(BLK, dtype=jnp.int32)[None, :]
    on_diag = row_ids == col_ids
    matrix = jnp.where(on_diag, diagonal, off_diag)
    return matrix.reshape(N_TRACT, NB, 2 * BLK * BLK).astype(jnp.bfloat16)


def with_ends(drawn, stream_key, least, high):
    spot = [jax.random.randint(jax.random.fold_in(stream_key, axis), (), 0, length) for axis, length in enumerate(drawn.shape)]
    main_axis = drawn.shape.index(max(drawn.shape))
    next_to = spot[:main_axis] + [(spot[main_axis] + 1) % drawn.shape[main_axis]] + spot[main_axis + 1:]
    return drawn.at[tuple(spot)].set(least).at[tuple(next_to)].set(high)


def level_of(stream_key, dims, cuts, low, largest):
    def one(position, blocks):
        heights = jax.random.uniform(jax.random.fold_in(jax.random.fold_in(stream_key, 6), position), (blocks,), jnp.float32, low / len(cuts), largest / len(cuts))
        return jnp.repeat(jnp.exp(heights), dims[position] // blocks).reshape((-1,) + (1,) * (len(dims) - position - 1))

    loudness = one(*cuts[0])
    for cut in cuts[1:]:
        loudness = loudness * one(*cut)
    return loudness


def deal_out(own_key, own, number, rows, amount, top, reach, slope):
    sequence = jax.random.permutation(own_key, amount)
    packed, usual = portions_of(amount, rows * top, reach, slope, True), portions_of(amount, rows * top, reach, slope, False)
    places = jnp.arange(amount)

    def named(lengths, offset_by):
        used = int((lengths > 0).sum())
        fixed = max(1, used // 4)
        moved = fixed + (places - fixed + offset_by * (used - fixed)) % max(1, amount - fixed)
        return jnp.zeros((amount,), jnp.int32).at[sequence[jnp.where(places < fixed, places, moved)]].set(jnp.asarray(lengths, jnp.int32))

    lengths = jnp.where(number % 4 == 0, named(packed, number // 4), named(usual, number - number // 4 - 1))
    mixed = jax.random.permutation(jax.random.fold_in(own, 3), amount)
    giver, sink = mixed[0:amount // 2 * 2:2], mixed[1:amount // 2 * 2:2]
    margin = jnp.minimum(lengths[giver] - 1, reach - lengths[sink]) // 2
    margin = jnp.where((giver == sequence[0]) | (sink == sequence[0]) | (lengths[sink] == 0), 0, jnp.maximum(margin, 0))
    moved = jax.random.randint(jax.random.fold_in(own, 4), (amount // 2,), 0, 1 << 20) % (margin + 1)
    lengths = lengths.at[giver].add(-moved).at[sink].add(moved)
    members = jnp.searchsorted(jnp.cumsum(lengths), jnp.arange(rows * top), side="right").astype(jnp.int32)
    table = members.reshape(top, rows).T
    table = table[jax.random.permutation(jax.random.fold_in(own, 1), rows)]
    offset_by = jax.random.randint(jax.random.fold_in(own, 2), (rows, 1), 0, top)
    return jnp.take_along_axis(table, (jnp.arange(top)[None, :] + offset_by) % top, axis=1)


def portions_of(amount, total, limit, lean, full):
    portions = [(1 << 20) // math.isqrt(standing ** lean) + 1 for standing in range(1, amount + 1)]
    largest = limit if full else min(limit, max(-(-total // amount), total * portions[0] // sum(portions)))
    least = 1 if total - largest >= amount - 1 else 0
    holding, spare = [largest] + [least] * (amount - 1), total - largest - least * (amount - 1)
    while spare > 0:
        candidates = [i for i in range(1, amount) if holding[i] < largest] or [i for i in range(1, amount) if holding[i] < limit]
        pool, left = sum([portions[i] for i in candidates]), spare
        for i in candidates:
            extra = min(limit - holding[i], max(1, left * portions[i] // pool), spare)
            holding[i] = holding[i] + extra
            spare = spare - extra
    return np.array(holding)


def normal_values(rng, shape, scale, bound, shards=(), kind=jnp.bfloat16):
    values = scale * jax.random.normal(rng, shape, jnp.float32)
    if shards:
        values = values * level_of(rng, shape, shards, -0.22, 0.18)
    return jnp.clip(values, -bound, bound).astype(kind)


def setup_inputs(seed: int = 0) -> dict:
    keys = jax.random.split(jax.random.key(seed), 8)
    images = normal_values(keys[0], (N_TRACT, NB, BLKIN * BLKIN), 1.0, 6.0, ((0, 8), (1, 64)))
    coefficients = normal_values(keys[1], (N_TRACT, NB, NBASIS * NTERMS), 0.5, 3.0, ((0, 8), (1, 64)))
    orders = with_ends(jax.random.randint(keys[2], (N_TRACT, NB), 0, 3), jax.random.fold_in(keys[2], 1), 0, 2).astype(jnp.int32)
    resample = draw_resample(jax.random.fold_in(keys[7], 71), 0)
    weights = jnp.clip(jnp.exp(math.log(0.5) - 2.306499 * jax.random.uniform(keys[4], (N_TRACT, NB), jnp.float32) ** level_of(keys[4], (N_TRACT, NB), ((0, 8), (1, 64)), -0.2, 0.2)), 0.049804688, 0.5).astype(jnp.bfloat16)
    routes_keys = jax.random.split(jax.random.fold_in(keys[5], 1), N_TRACT * NB // B_DEV)
    routes_turns = jax.random.permutation(jax.random.fold_in(keys[5], 3), N_TRACT * NB // B_DEV)
    routes = jax.vmap(lambda own, number: deal_out(jax.random.fold_in(keys[5], 2), own, number, B_DEV, N_VISIT, TOP, CAP, 2))(routes_keys, routes_turns).reshape((N_TRACT, NB, TOP))
    offsets = with_ends(jax.random.randint(keys[6], (N_TRACT, NB, TOP, 2), 0, PATCH - BLK + 1), jax.random.fold_in(keys[6], 1), 0, PATCH - BLK).astype(jnp.int32)
    return {"images": images, "coefficients": coefficients, "orders": orders, "resample": resample, "weights": weights, "routes": routes, "offsets": offsets}


SIGMAS = (0.7, 1.5, 3.0, 2.0)
POWERS = (0, 0, 0, 1)
TERM_DEGREES = (0, 1, 1, 2, 2, 2)


def kernel_tables():
    row_ids = jnp.arange(BLK, dtype=jnp.int32)[:, None]
    col_ids = jnp.arange(BLKIN, dtype=jnp.int32)[None, :]
    difference = col_ids - row_ids
    inside = (difference >= 0) & (difference < KSIZE)
    shifted = difference.astype(jnp.float32) - jnp.float32(HALF)
    tap_offsets = jnp.arange(KSIZE, dtype=jnp.float32) - jnp.float32(HALF)
    tables = []
    for spread_sigma, degree_power in zip(SIGMAS, POWERS):
        def profile(offset):
            shape_value = jnp.exp(-offset * offset / (2.0 * spread_sigma * spread_sigma))
            if degree_power == 1:
                shape_value = shape_value * offset / spread_sigma
            return shape_value
        normal_sum = jnp.sum(jnp.abs(profile(tap_offsets)))
        tables.append(jnp.where(inside, profile(shifted) / normal_sum, jnp.float32(0.0)))
    return jnp.stack(tables).astype(jnp.bfloat16)


def monomial_planes():
    centres = (2.0 * jnp.arange(BLK, dtype=jnp.float32) + 1.0) / BLK - 1.0
    across = centres[:, None] * jnp.ones((1, BLK), jnp.float32)
    downward = jnp.ones((BLK, 1), jnp.float32) * centres[None, :]
    ones_plane = jnp.ones((BLK, BLK), jnp.float32)
    return jnp.stack([ones_plane, across, downward, across * across, across * downward, downward * downward])


def mask_coefficients(coefficients, orders):
    shaped = coefficients.reshape(orders.shape + (NBASIS, NTERMS))
    degrees = jnp.array(TERM_DEGREES, jnp.int32)
    keep = degrees <= orders[..., None, None]
    return jnp.where(keep, shaped, jnp.zeros_like(shaped))


def match_and_warp(images, masked, resample, tables, monomials):
    batch_size = images.shape[0]
    accumulated = jnp.zeros((batch_size, BLK, BLK), jnp.float32)
    tables_wide = tables.astype(jnp.float32)
    images_wide = images.astype(jnp.float32)
    for row_kernel in range(4):
        smooth = jnp.einsum('ix,nxy->niy', tables_wide[row_kernel], images_wide).astype(jnp.bfloat16)
        smooth_wide = smooth.astype(jnp.float32)
        for col_kernel in range(4):
            response = jnp.einsum('niy,jy->nij', smooth_wide, tables_wide[col_kernel])
            factor = masked[:, 4 * row_kernel + col_kernel, :].astype(jnp.float32)
            spatial = factor[:, 0, None, None] * monomials[0]
            for monomial in range(1, NTERMS):
                spatial = spatial + factor[:, monomial, None, None] * monomials[monomial]
            accumulated = accumulated + spatial * response
    matched = accumulated.astype(jnp.bfloat16).astype(jnp.float32)
    rows_matrix = resample[:, 0].astype(jnp.float32)
    cols_matrix = resample[:, 1].astype(jnp.float32)
    halfway = jnp.einsum('nij,njk->nik', rows_matrix, matched).astype(jnp.bfloat16).astype(jnp.float32)
    return jnp.einsum('nik,nlk->nil', halfway, cols_matrix).astype(jnp.bfloat16)


def reference(images, coefficients, orders, resample, weights, routes, offsets):
    tables = kernel_tables()
    monomials = monomial_planes()
    masked = mask_coefficients(coefficients, orders)
    group_size = 128
    grouped = (images.reshape(-1, group_size, BLKIN, BLKIN),
               masked.reshape(-1, group_size, NBASIS, NTERMS),
               resample.reshape(-1, group_size, 2, BLK, BLK))
    warped = lax.map(lambda pieces: match_and_warp(pieces[0], pieces[1], pieces[2], tables, monomials), grouped)
    warped = warped.reshape(-1, BLK, BLK)
    destination = routes.reshape(-1).astype(jnp.int32)
    row_offsets = offsets[..., 0].reshape(-1).astype(jnp.int32)
    col_offsets = offsets[..., 1].reshape(-1).astype(jnp.int32)
    block_weight = weights.reshape(-1).astype(jnp.float32)

    def add_pair(pair_index, running):
        coadd_flux, coadd_weight = running
        pair_index = jnp.asarray(pair_index).astype(jnp.int32)
        block_index = (pair_index // TOP).astype(jnp.int32)
        block = lax.dynamic_index_in_dim(warped, block_index, 0, keepdims=False).astype(jnp.float32)
        scale = lax.dynamic_index_in_dim(block_weight, block_index, 0, keepdims=False)
        corner = (destination[pair_index].astype(jnp.int32), row_offsets[pair_index].astype(jnp.int32), col_offsets[pair_index].astype(jnp.int32))
        previous = lax.dynamic_slice(coadd_flux, corner, (1, BLK, BLK))
        coadd_flux = lax.dynamic_update_slice(coadd_flux, previous + scale * block[None], corner)
        previous_weight = lax.dynamic_slice(coadd_weight, corner, (1, BLK, BLK))
        coadd_weight = lax.dynamic_update_slice(coadd_weight, previous_weight + scale, corner)
        return (coadd_flux, coadd_weight)

    empty = jnp.zeros((N_VISIT, PATCH, PATCH), jnp.float32)
    coadd_flux, coadd_weight = lax.fori_loop(0, destination.shape[0], add_pair, (empty, empty))
    return coadd_flux, coadd_weight
```

```python
import jax
import jax.numpy as jnp
from jax import lax
from jax.sharding import PartitionSpec as P

KSIZE = 41
NBASIS = 16
NTERMS = 6
TOP = 2
BLK = 40
PATCH = 256
HALF = 20
BLKIN = 80


SIGMAS = (0.7, 1.5, 3.0, 2.0)
POWERS = (0, 0, 0, 1)
TERM_DEGREES = (0, 1, 1, 2, 2, 2)


def kernel_tables():
    row_ids = jnp.arange(BLK, dtype=jnp.int32)[:, None]
    col_ids = jnp.arange(BLK + KSIZE - 1, dtype=jnp.int32)[None, :]
    difference = col_ids - row_ids
    inside = (difference >= 0) & (difference < KSIZE)
    shifted = difference.astype(jnp.float32) - jnp.float32(HALF)
    tap_offsets = jnp.arange(KSIZE, dtype=jnp.float32) - jnp.float32(HALF)
    tables = []
    for spread_sigma, degree_power in zip(SIGMAS, POWERS):

        def profile(offset):
            shape_value = jnp.exp(-offset * offset / (2.0 * spread_sigma * spread_sigma))
            if degree_power == 1:
                shape_value = shape_value * offset / spread_sigma
            return shape_value

        normal_sum = jnp.sum(jnp.abs(profile(tap_offsets)))
        tables.append(jnp.where(inside, profile(shifted) / normal_sum, jnp.float32(0.0)))
    return jnp.stack(tables).astype(jnp.bfloat16)


def monomial_planes():
    centres = (2.0 * jnp.arange(BLK, dtype=jnp.float32) + 1.0) / BLK - 1.0
    across = centres[:, None] * jnp.ones((1, BLK), jnp.float32)
    downward = jnp.ones((BLK, 1), jnp.float32) * centres[None, :]
    ones_plane = jnp.ones((BLK, BLK), jnp.float32)
    return jnp.stack(
        [ones_plane, across, downward, across * across, across * downward, downward * downward]
    )


def mask_coefficients(coefficients, orders):
    shaped = coefficients.reshape(orders.shape + (NBASIS, NTERMS))
    degrees = jnp.array(TERM_DEGREES, jnp.int32)
    keep = degrees <= orders[..., None, None]
    return jnp.where(keep, shaped, jnp.zeros_like(shaped))


def match_and_warp(flat_images, masked, flat_resample, tables, monomials):
    images = flat_images.reshape(-1, BLKIN, BLKIN)
    resample = flat_resample.reshape(-1, 2, BLK, BLK)
    batch_size = images.shape[0]
    accumulated = jnp.zeros((batch_size, BLK, BLK), jnp.float32)
    for row_kernel in range(4):
        smooth = jnp.einsum(
            "ix,nxy->niy", tables[row_kernel], images, preferred_element_type=jnp.float32
        ).astype(jnp.bfloat16)
        for col_kernel in range(4):
            response = jnp.einsum(
                "niy,jy->nij", smooth, tables[col_kernel], preferred_element_type=jnp.float32
            )
            factor = masked[:, 4 * row_kernel + col_kernel, :].astype(jnp.float32)
            spatial = factor[:, 0, None, None] * monomials[0]
            for monomial in range(1, NTERMS):
                spatial = spatial + factor[:, monomial, None, None] * monomials[monomial]
            accumulated = accumulated + spatial * response
    matched = accumulated.astype(jnp.bfloat16)
    halfway = jnp.einsum(
        "nij,njk->nik", resample[:, 0], matched, preferred_element_type=jnp.float32
    ).astype(jnp.bfloat16)
    return jnp.einsum(
        "nik,nlk->nil", halfway, resample[:, 1], preferred_element_type=jnp.float32
    ).astype(jnp.bfloat16)


WIDTH = 1664


def per_device(images, coefficients, orders, resample, weights, routes, offsets):
    tables = kernel_tables()
    monomials = monomial_planes()
    masked = mask_coefficients(coefficients[0], orders[0])
    block_count = images.shape[1]
    visit_count = lax.axis_size("visit")
    tract_count = lax.axis_size("tract")
    capacity = max(2, 4 * block_count // visit_count)
    pair_count = block_count * TOP
    slot_count = visit_count * capacity
    warped_here = match_and_warp(images[0], masked, resample[0], tables, monomials)
    destination = routes[0].reshape(pair_count)
    pair_ids = jnp.arange(pair_count, dtype=jnp.int32)
    same_patch = destination[:, None] == destination[None, :]
    earlier = pair_ids[None, :] < pair_ids[:, None]
    slot_rank = jnp.sum((same_patch & earlier).astype(jnp.int32), axis=1)
    slot_index = destination * capacity + slot_rank
    slot_pick = (jnp.arange(slot_count, dtype=jnp.int32)[:, None] == slot_index[None, :]).astype(
        jnp.bfloat16
    )
    slot_owner = (
        pair_ids[:, None] // TOP == jnp.arange(block_count, dtype=jnp.int32)[None, :]
    ).astype(jnp.bfloat16)
    choose = jnp.dot(slot_pick, slot_owner, preferred_element_type=jnp.float32).astype(jnp.bfloat16)
    pair_weight = jnp.repeat(weights[0], TOP)
    pair_offsets = offsets[0].reshape(pair_count, 2).astype(jnp.bfloat16)
    extras = jnp.concatenate([pair_offsets, pair_weight[:, None]], axis=1)
    slot_extras = jnp.dot(slot_pick, extras, preferred_element_type=jnp.float32).astype(
        jnp.bfloat16
    )
    slot_warped = jnp.dot(
        choose, warped_here.reshape(block_count, BLK * BLK), preferred_element_type=jnp.float32
    ).astype(jnp.bfloat16)
    parcel = jnp.concatenate([slot_warped, slot_extras], axis=1)
    parcel = jnp.pad(parcel, ((0, 0), (0, WIDTH - parcel.shape[1])))
    parcel = lax.all_to_all(
        parcel.reshape(visit_count, capacity, WIDTH), "visit", split_axis=0, concat_axis=0, tiled=True
    ).reshape(slot_count, WIDTH)
    warped = parcel[:, : BLK * BLK].reshape(slot_count, BLK, BLK)
    arrived = parcel[:, BLK * BLK : BLK * BLK + 3]
    pixels = jnp.arange(PATCH, dtype=jnp.float32)
    within = jnp.arange(BLK, dtype=jnp.float32)
    row_hit = (
        pixels[None, None, :]
        == arrived[:, 0, None, None].astype(jnp.float32) + within[None, :, None]
    )
    col_hit = (
        pixels[None, None, :]
        == arrived[:, 1, None, None].astype(jnp.float32) + within[None, :, None]
    )
    row_place = jnp.where(row_hit, arrived[:, 2, None, None], jnp.zeros((), jnp.bfloat16))
    col_place = col_hit.astype(jnp.bfloat16)
    spread = jnp.einsum(
        "sij,sjq->siq", warped, col_place, preferred_element_type=jnp.float32
    ).astype(jnp.bfloat16)
    partial = jnp.einsum("sip,siq->pq", row_place, spread, preferred_element_type=jnp.float32)
    row_cover = jnp.sum(row_place.astype(jnp.float32), axis=1).astype(jnp.bfloat16)
    col_cover = jnp.sum(col_place.astype(jnp.float32), axis=1).astype(jnp.bfloat16)
    partial_weight = jnp.einsum(
        "sp,sq->pq", row_cover, col_cover, preferred_element_type=jnp.float32
    )
    rows = PATCH // tract_count
    both = jnp.concatenate(
        [partial.reshape(tract_count, rows, PATCH), partial_weight.reshape(tract_count, rows, PATCH)],
        axis=1,
    ).astype(jnp.bfloat16)
    both = lax.all_to_all(both, "tract", split_axis=0, concat_axis=0, tiled=True)
    sums = jnp.sum(both.astype(jnp.float32), axis=0)
    return (sums[None, :rows], sums[None, rows:])


def solution(mesh):
    in_specs = (
        P("tract", "visit", None),
        P("tract", "visit", None),
        P("tract", "visit"),
        P("tract", "visit", None),
        P("tract", "visit"),
        P("tract", "visit", None),
        P("tract", "visit", None, None),
    )
    out_specs = (P("visit", "tract", None), P("visit", "tract", None))
    return jax.shard_map(
        per_device, mesh=mesh, in_specs=in_specs, out_specs=out_specs, check_vma=False
    )
```

```python
import functools

import jax
import jax.numpy as jnp
import numpy as np
from jax import lax
from jax.experimental import pallas as pl
from jax.experimental.pallas import tpu as pltpu
from jax.sharding import PartitionSpec as P

KSIZE = 41
NBASIS = 16
NTERMS = 6
TOP = 2
BLK = 40
PATCH = 256
HALF = 20
BLKIN = 80
LANES = 128
WIDTH = 1664
EXTRA = 1600 % LANES

SIGMAS = (0.7, 1.5, 3.0, 2.0)
POWERS = (0, 0, 0, 1)
COLUMN_AT = (0, 40, 80, 128)


def constant_tables():
    difference = np.arange(BLKIN)[None, :] - np.arange(BLK)[:, None]
    inside = (difference >= 0) & (difference < KSIZE)
    shifted = (difference - HALF).astype(np.float32)
    taps = np.arange(KSIZE, dtype=np.float32) - np.float32(HALF)
    tables = []
    for sigma, power in zip(SIGMAS, POWERS):

        def profile(offset):
            value = np.exp(-offset * offset / np.float32(2.0 * sigma * sigma)).astype(np.float32)
            if power == 1:
                value = value * offset / np.float32(sigma)
            return value.astype(np.float32)

        total = np.sum(np.abs(profile(taps)), dtype=np.float32)
        tables.append(np.where(inside, profile(shifted) / total, np.float32(0.0)))
    centres = ((2.0 * np.arange(BLK, dtype=np.float32) + 1.0) / BLK - 1.0).astype(np.float32)
    row_tables = np.concatenate(tables, axis=0)
    column_tables = np.zeros((LANES, 2 * LANES), np.float32)
    spread = np.zeros((4 * NTERMS, NTERMS, 2 * LANES), np.float32)
    across = np.zeros((8, 2 * LANES), np.float32)
    for c, at in enumerate(COLUMN_AT):
        column_tables[:BLKIN, at : at + BLK] = tables[c].T
        across[:, at : at + BLK] = centres
        for m in range(NTERMS):
            spread[c * NTERMS + m, m, at : at + BLK] = 1.0
    return (
        jnp.asarray(row_tables, jnp.bfloat16),
        jnp.asarray(column_tables, jnp.bfloat16),
        jnp.asarray(spread.reshape(4 * NTERMS, NTERMS * 2 * LANES), jnp.bfloat16),
        jnp.asarray(across),
    )


def warp_kernel(
    images_ref,
    coefficients_ref,
    orders_ref,
    resample_ref,
    weights_ref,
    routes_ref,
    offsets_ref,
    row_tables_ref,
    column_tables_ref,
    spread_ref,
    across_ref,
    out_ref,
    image_rows,
    resample_rows,
    planes,
    warped_rows,
    flat,
):
    f32, bf16 = jnp.float32, jnp.bfloat16
    blocks = images_ref.shape[0]
    group = 4
    wide = 2 * LANES

    for x in range(BLKIN):
        start = min(x * BLKIN, BLKIN * BLKIN - LANES)
        piece = images_ref[:, start : start + LANES].astype(f32)
        if start != x * BLKIN:
            piece = jnp.roll(piece, start - x * BLKIN, axis=1)
        image_rows[pl.ds(x, blocks, stride=BLKIN), :] = piece
        start = min(x * BLK, 2 * BLK * BLK - LANES)
        piece = resample_ref[:, start : start + LANES].astype(f32)
        if start != x * BLK:
            piece = jnp.roll(piece, start - x * BLK, axis=1)
        resample_rows[pl.ds(x, blocks, stride=2 * BLK), :] = piece

    terms = jnp.concatenate(
        [coefficients_ref[:, 4 * NTERMS * r : 4 * NTERMS * (r + 1)] for r in range(4)], axis=0
    )
    spread = jnp.dot(terms, spread_ref[...], preferred_element_type=f32)
    lane = lax.broadcasted_iota(jnp.int32, (blocks, blocks), 1)
    sublane = lax.broadcasted_iota(jnp.int32, (blocks, blocks), 0)
    order = jnp.sum(
        jnp.where(lane == sublane, orders_ref[...].astype(f32), 0.0), axis=1, keepdims=True
    )
    order = jnp.concatenate([order] * 4, axis=0)
    first, second = order >= 1.0, order >= 2.0
    term = [spread[:, wide * m : wide * (m + 1)] for m in range(NTERMS)]
    term = (
        term[:1]
        + [jnp.where(first, t, 0.0) for t in term[1:3]]
        + [jnp.where(second, t, 0.0) for t in term[3:]]
    )
    across = across_ref[0:1, :]
    planes[:, :wide] = term[0] + across * (term[2] + across * term[5])
    planes[:, wide : 2 * wide] = term[1] + across * term[4]
    planes[:, 2 * wide :] = term[3]

    row_id = lax.broadcasted_iota(jnp.int32, (BLK, wide), 0).astype(f32)
    down = (2.0 * row_id + 1.0) / BLK - 1.0

    def step(number, _):
        first_block = number * group
        stacked = jnp.concatenate(
            [
                image_rows[pl.ds(pl.multiple_of((first_block + g) * BLKIN, 8), BLKIN), :]
                for g in range(group)
            ],
            axis=1,
        ).astype(bf16)
        smooth = jnp.dot(row_tables_ref[...], stacked, preferred_element_type=f32).astype(bf16)
        for g in range(group):
            block = first_block + g
            response = jnp.dot(
                smooth[:, LANES * g : LANES * (g + 1)],
                column_tables_ref[...],
                preferred_element_type=f32,
            )
            total = jnp.zeros((BLK, wide), f32)
            for r in range(4):
                plane = planes[pl.ds(r * blocks + block, 1), :]
                weight = plane[:, :wide] + down * (
                    plane[:, wide : 2 * wide] + down * plane[:, 2 * wide :]
                )
                total = total + weight * response[BLK * r : BLK * (r + 1), :]
            low, high = total[:, :LANES], total[:, LANES:]
            folded = (
                low
                + high
                + pltpu.roll(low, LANES - BLK, axis=1)
                + pltpu.roll(low, LANES - 2 * BLK, axis=1)
            )
            matched = folded[:, :BLK].astype(bf16)
            at = pl.multiple_of(block * 2 * BLK, 8)
            left = resample_rows[pl.ds(at, BLK), :][:, :BLK].astype(bf16)
            right = resample_rows[pl.ds(at + BLK, BLK), :][:, :BLK].astype(bf16)
            halfway = jnp.dot(left, matched, preferred_element_type=f32).astype(bf16)
            warped = lax.dot_general(
                halfway, right, (((1,), (1,)), ((), ())), preferred_element_type=f32
            )
            warped_rows[pl.ds(pl.multiple_of(block * BLK, 8), BLK), 0:BLK] = warped
        return 0

    lax.fori_loop(0, blocks // group, step, 0)

    flat[:, 12 * LANES :] = jnp.zeros((blocks, LANES), f32)
    for i in range(BLK):
        flat[:, BLK * i : BLK * (i + 1)] = warped_rows[pl.ds(i, blocks, stride=BLK), 0:BLK]
    pixels = flat[...].astype(bf16)

    slots, pairs = out_ref.shape[0], TOP * blocks
    patch = jnp.concatenate([routes_ref[k : k + 1, :] for k in range(TOP)], axis=1)
    slot = lax.broadcasted_iota(jnp.int32, (slots, pairs), 0)
    hit = jnp.where(patch == slot // 2, 1.0, 0.0)
    before = lax.broadcasted_iota(jnp.int32, (pairs, pairs), 0)
    after = lax.broadcasted_iota(jnp.int32, (pairs, pairs), 1)
    rank = jnp.dot(
        hit.astype(bf16),
        jnp.where(before < after, 1.0, 0.0).astype(bf16),
        preferred_element_type=f32,
    )
    pick = jnp.where(rank == (slot % 2).astype(f32), hit, 0.0).astype(bf16)
    packed = jnp.dot(
        pick, jnp.concatenate([pixels] * TOP, axis=0), preferred_element_type=f32
    )
    column = lax.broadcasted_iota(jnp.int32, (LANES, pairs), 0) - EXTRA
    corner_y = jnp.concatenate([offsets_ref[k, 0:1, :] for k in range(TOP)], axis=1).astype(f32)
    corner_x = jnp.concatenate([offsets_ref[k, 1:2, :] for k in range(TOP)], axis=1).astype(f32)
    weight = jnp.concatenate([weights_ref[...].astype(f32)] * TOP, axis=1)
    extras = jnp.where(
        column == 0,
        corner_y,
        jnp.where(column == 1, corner_x, jnp.where(column == 2, weight, 0.0)),
    ).astype(bf16)
    tail = lax.dot_general(pick, extras, (((1,), (1,)), ((), ())), preferred_element_type=f32)
    out_ref[:, : 12 * LANES] = packed[:, : 12 * LANES].astype(bf16)
    out_ref[:, 12 * LANES :] = (packed[:, 12 * LANES :] + tail).astype(bf16)


def warp_and_pack(images, coefficients, orders, resample, weights, routes, offsets, slots):
    blocks = images.shape[0]
    f32 = jnp.float32
    return pl.pallas_call(
        warp_kernel,
        out_shape=jax.ShapeDtypeStruct((slots, WIDTH), jnp.bfloat16),
        scratch_shapes=[
            pltpu.VMEM((blocks * BLKIN, LANES), f32),
            pltpu.VMEM((blocks * 2 * BLK, LANES), f32),
            pltpu.VMEM((blocks * 4, 3 * 2 * LANES), f32),
            pltpu.VMEM((blocks * BLK, LANES), f32),
            pltpu.VMEM((blocks, WIDTH), f32),
        ],
        compiler_params=pltpu.CompilerParams(vmem_limit_bytes=32 << 20),
        name="warp_and_pack",
    )(
        images,
        coefficients,
        orders,
        resample,
        weights,
        jnp.transpose(routes, (1, 0)),
        jnp.transpose(offsets, (1, 2, 0)),
        *constant_tables(),
    )


def per_device(images, coefficients, orders, resample, weights, routes, offsets):
    visit_count = lax.axis_size("visit")
    tract_count = lax.axis_size("tract")
    capacity = 2
    slot_count = visit_count * capacity
    parcel = warp_and_pack(
        images[0],
        coefficients[0],
        orders,
        resample[0],
        weights,
        routes[0],
        offsets[0],
        slot_count,
    )
    parcel = lax.all_to_all(
        parcel.reshape(visit_count, capacity, WIDTH), "visit", split_axis=0, concat_axis=0, tiled=True
    ).reshape(slot_count, WIDTH)
    warped = parcel[:, : BLK * BLK].reshape(slot_count, BLK, BLK)
    arrived = parcel[:, BLK * BLK : BLK * BLK + 3]
    pixels = jnp.arange(PATCH, dtype=jnp.float32)
    within = jnp.arange(BLK, dtype=jnp.float32)
    row_hit = (
        pixels[None, None, :]
        == arrived[:, 0, None, None].astype(jnp.float32) + within[None, :, None]
    )
    col_hit = (
        pixels[None, None, :]
        == arrived[:, 1, None, None].astype(jnp.float32) + within[None, :, None]
    )
    row_place = jnp.where(row_hit, arrived[:, 2, None, None], jnp.zeros((), jnp.bfloat16))
    col_place = col_hit.astype(jnp.bfloat16)
    spread = jnp.einsum(
        "sij,sjq->siq", warped, col_place, preferred_element_type=jnp.float32
    ).astype(jnp.bfloat16)
    partial = jnp.einsum("sip,siq->pq", row_place, spread, preferred_element_type=jnp.float32)
    row_cover = jnp.sum(row_place.astype(jnp.float32), axis=1).astype(jnp.bfloat16)
    col_cover = jnp.sum(col_place.astype(jnp.float32), axis=1).astype(jnp.bfloat16)
    partial_weight = jnp.einsum(
        "sp,sq->pq", row_cover, col_cover, preferred_element_type=jnp.float32
    )
    rows = PATCH // tract_count
    both = jnp.concatenate(
        [partial.reshape(tract_count, rows, PATCH), partial_weight.reshape(tract_count, rows, PATCH)],
        axis=1,
    ).astype(jnp.bfloat16)
    both = lax.all_to_all(both, "tract", split_axis=0, concat_axis=0, tiled=True)
    sums = jnp.sum(both.astype(jnp.float32), axis=0)
    return (sums[None, :rows], sums[None, rows:])


def solution(mesh):
    in_specs = (
        P("tract", "visit", None),
        P("tract", "visit", None),
        P("tract", "visit"),
        P("tract", "visit", None),
        P("tract", "visit"),
        P("tract", "visit", None),
        P("tract", "visit", None, None),
    )
    out_specs = (P("visit", "tract", None), P("visit", "tract", None))
    return jax.shard_map(
        per_device, mesh=mesh, in_specs=in_specs, out_specs=out_specs, check_vma=False
    )
```

```python
import functools

import jax
import jax.numpy as jnp
import numpy as np
from jax import lax
from jax.experimental import pallas as pl
from jax.experimental.pallas import tpu as pltpu
from jax.sharding import PartitionSpec as P

KSIZE = 41
NBASIS = 16
NTERMS = 6
TOP = 2
BLK = 40
PATCH = 256
HALF = 20
BLKIN = 80
LANES = 128
WIDTH = 1664
EXTRA = 1600 % LANES

SIGMAS = (0.7, 1.5, 3.0, 2.0)
POWERS = (0, 0, 0, 1)
COLUMN_AT = (0, 40, 80, 128)


def constant_tables():
    difference = np.arange(BLKIN)[None, :] - np.arange(BLK)[:, None]
    inside = (difference >= 0) & (difference < KSIZE)
    shifted = (difference - HALF).astype(np.float32)
    taps = np.arange(KSIZE, dtype=np.float32) - np.float32(HALF)
    tables = []
    for sigma, power in zip(SIGMAS, POWERS):

        def profile(offset):
            value = np.exp(-offset * offset / np.float32(2.0 * sigma * sigma)).astype(np.float32)
            if power == 1:
                value = value * offset / np.float32(sigma)
            return value.astype(np.float32)

        total = np.sum(np.abs(profile(taps)), dtype=np.float32)
        tables.append(np.where(inside, profile(shifted) / total, np.float32(0.0)))
    centres = ((2.0 * np.arange(BLK, dtype=np.float32) + 1.0) / BLK - 1.0).astype(np.float32)
    row_tables = np.concatenate(tables, axis=0)
    column_tables = np.zeros((LANES, 2 * LANES), np.float32)
    spread = np.zeros((4 * NTERMS, NTERMS, 2 * LANES), np.float32)
    across = np.zeros((8, 2 * LANES), np.float32)
    for c, at in enumerate(COLUMN_AT):
        column_tables[:BLKIN, at : at + BLK] = tables[c].T
        across[:, at : at + BLK] = centres
        for m in range(NTERMS):
            spread[c * NTERMS + m, m, at : at + BLK] = 1.0
    return (
        jnp.asarray(row_tables, jnp.bfloat16),
        jnp.asarray(column_tables, jnp.bfloat16),
        jnp.asarray(spread.reshape(4 * NTERMS, NTERMS * 2 * LANES), jnp.bfloat16),
        jnp.asarray(across),
    )


def warp_kernel(
    images_ref,
    coefficients_ref,
    orders_ref,
    resample_ref,
    weights_ref,
    routes_ref,
    offsets_ref,
    row_tables_ref,
    column_tables_ref,
    spread_ref,
    across_ref,
    out_ref,
    image_rows,
    resample_rows,
    planes,
    warped_rows,
    flat,
    *held,
):
    f32, bf16 = jnp.float32, jnp.bfloat16
    *held, arrival = held
    sources = (
        images_ref,
        resample_ref,
        coefficients_ref,
        orders_ref,
        weights_ref,
        routes_ref,
        offsets_ref,
        row_tables_ref,
        column_tables_ref,
        spread_ref,
        across_ref,
    )
    copies = [
        pltpu.make_async_copy(source, kept, arrival.at[number])
        for number, (source, kept) in enumerate(zip(sources, held, strict=True))
    ]
    for copy in copies:
        copy.start()
    (
        images_ref,
        resample_ref,
        coefficients_ref,
        orders_ref,
        weights_ref,
        routes_ref,
        offsets_ref,
        row_tables_ref,
        column_tables_ref,
        spread_ref,
        across_ref,
    ) = held
    for copy in copies[2:]:
        copy.wait()
    copies[0].wait()
    blocks = images_ref.shape[0]
    wide = 2 * LANES

    for x in range(BLKIN):
        start = min(x * BLKIN, BLKIN * BLKIN - LANES)
        piece = images_ref[:, start : start + LANES].astype(f32)
        if start != x * BLKIN:
            piece = jnp.roll(piece, start - x * BLKIN, axis=1)
        image_rows[pl.ds(x, blocks, stride=BLKIN + 1), :] = piece
    copies[1].wait()
    for x in range(2 * BLK):
        start = min(x * BLK, 2 * BLK * BLK - LANES)
        piece = resample_ref[:, start : start + LANES].astype(f32)
        if start != x * BLK:
            piece = jnp.roll(piece, start - x * BLK, axis=1)
        resample_rows[pl.ds(x, blocks, stride=2 * BLK + 1), :] = piece

    terms = jnp.concatenate(
        [coefficients_ref[:, 4 * NTERMS * r : 4 * NTERMS * (r + 1)] for r in range(4)], axis=0
    )
    spread = jnp.dot(terms, spread_ref[...], preferred_element_type=f32)
    lane = lax.broadcasted_iota(jnp.int32, (blocks, blocks), 1)
    sublane = lax.broadcasted_iota(jnp.int32, (blocks, blocks), 0)
    order = jnp.sum(
        jnp.where(lane == sublane, orders_ref[...].astype(f32), 0.0), axis=1, keepdims=True
    )
    order = jnp.concatenate([order] * 4, axis=0)
    first, second = order >= 1.0, order >= 2.0
    term = [spread[:, wide * m : wide * (m + 1)] for m in range(NTERMS)]
    term = (
        term[:1]
        + [jnp.where(first, t, 0.0) for t in term[1:3]]
        + [jnp.where(second, t, 0.0) for t in term[3:]]
    )
    across = across_ref[0:1, :]
    planes[:, :wide] = term[0] + across * (term[2] + across * term[5])
    planes[:, wide : 2 * wide] = term[1] + across * term[4]
    planes[:, 2 * wide :] = term[3]

    row_id = lax.broadcasted_iota(jnp.int32, (BLK, wide), 0).astype(f32)
    down = (2.0 * row_id + 1.0) / BLK - 1.0

    stacked = jnp.concatenate(
        [
            image_rows[(BLKIN + 1) * g : (BLKIN + 1) * g + BLKIN, :]
            for g in range(blocks)
        ],
        axis=1,
    ).astype(bf16)
    smooth = jnp.dot(row_tables_ref[...], stacked, preferred_element_type=f32).astype(bf16)
    responses = [
        jnp.dot(
            smooth[:, LANES * g : LANES * (g + 1)],
            column_tables_ref[...],
            preferred_element_type=f32,
        )
        for g in range(blocks)
    ]
    matched = []
    for g in range(blocks):
        total = jnp.zeros((BLK, wide), f32)
        for r in range(4):
            plane = planes[r * blocks + g : r * blocks + g + 1, :]
            weight = plane[:, :wide] + down * (
                plane[:, wide : 2 * wide] + down * plane[:, 2 * wide :]
            )
            total = total + weight * responses[g][BLK * r : BLK * (r + 1), :]
        low, high = total[:, :LANES], total[:, LANES:]
        folded = (
            low
            + high
            + pltpu.roll(low, LANES - BLK, axis=1)
            + pltpu.roll(low, LANES - 2 * BLK, axis=1)
        )
        matched.append(folded[:, :BLK].astype(bf16))
    halfway = [
        jnp.dot(
            resample_rows[(2 * BLK + 1) * g : (2 * BLK + 1) * g + BLK, :][:, :BLK].astype(bf16),
            matched[g],
            preferred_element_type=f32,
        ).astype(bf16)
        for g in range(blocks)
    ]
    warped = [
        lax.dot_general(
            halfway[g],
            resample_rows[(2 * BLK + 1) * g + BLK : (2 * BLK + 1) * (g + 1) - 1, :][:, :BLK].astype(bf16),
            (((1,), (1,)), ((), ())),
            preferred_element_type=f32,
        )
        for g in range(blocks)
    ]
    for g in range(blocks):
        warped_rows[(BLK + 1) * g : (BLK + 1) * g + BLK, 0:BLK] = warped[g]
    flat[:, 12 * LANES :] = jnp.zeros((blocks, LANES), f32)
    for i in range(BLK):
        flat[:, BLK * i : BLK * (i + 1)] = warped_rows[pl.ds(i, blocks, stride=BLK + 1), 0:BLK]
    pixels = flat[...].astype(bf16)

    slots, pairs = out_ref.shape[0], TOP * blocks
    patch = jnp.concatenate([routes_ref[k : k + 1, :] for k in range(TOP)], axis=1)
    slot = lax.broadcasted_iota(jnp.int32, (slots, pairs), 0)
    hit = jnp.where(patch == slot // 2, 1.0, 0.0)
    before = lax.broadcasted_iota(jnp.int32, (pairs, pairs), 0)
    after = lax.broadcasted_iota(jnp.int32, (pairs, pairs), 1)
    rank = jnp.dot(
        hit.astype(bf16),
        jnp.where(before < after, 1.0, 0.0).astype(bf16),
        preferred_element_type=f32,
    )
    pick = jnp.where(rank == (slot % 2).astype(f32), hit, 0.0).astype(bf16)
    packed = jnp.dot(
        pick, jnp.concatenate([pixels] * TOP, axis=0), preferred_element_type=f32
    )
    column = lax.broadcasted_iota(jnp.int32, (LANES, pairs), 0) - EXTRA
    corner_y = jnp.concatenate([offsets_ref[k, 0:1, :] for k in range(TOP)], axis=1).astype(f32)
    corner_x = jnp.concatenate([offsets_ref[k, 1:2, :] for k in range(TOP)], axis=1).astype(f32)
    weight = jnp.concatenate([weights_ref[...].astype(f32)] * TOP, axis=1)
    extras = jnp.where(
        column == 0,
        corner_y,
        jnp.where(column == 1, corner_x, jnp.where(column == 2, weight, 0.0)),
    ).astype(bf16)
    tail = lax.dot_general(pick, extras, (((1,), (1,)), ((), ())), preferred_element_type=f32)
    out_ref[:, : 12 * LANES] = packed[:, : 12 * LANES].astype(bf16)
    out_ref[:, 12 * LANES :] = (packed[:, 12 * LANES :] + tail).astype(bf16)


def warp_and_pack(images, coefficients, orders, resample, weights, routes, offsets, slots):
    blocks = images.shape[0]
    f32 = jnp.float32
    operands = (
        images,
        coefficients,
        orders,
        resample,
        weights,
        jnp.transpose(routes, (1, 0)),
        jnp.transpose(offsets, (1, 2, 0)),
        *constant_tables(),
    )
    kept = [operands[n] for n in (0, 3, 1, 2, 4, 5, 6, 7, 8, 9, 10)]
    return pl.pallas_call(
        warp_kernel,
        out_shape=jax.ShapeDtypeStruct((slots, WIDTH), jnp.bfloat16),
        in_specs=[pl.BlockSpec(memory_space=pl.ANY)] * len(operands),
        scratch_shapes=[
            pltpu.VMEM((blocks * (BLKIN + 1), LANES), f32),
            pltpu.VMEM((blocks * (2 * BLK + 1), LANES), f32),
            pltpu.VMEM((blocks * 4, 3 * 2 * LANES), f32),
            pltpu.VMEM((blocks * (BLK + 1), LANES), f32),
            pltpu.VMEM((blocks, WIDTH), f32),
            *[pltpu.VMEM(array.shape, array.dtype) for array in kept],
            pltpu.SemaphoreType.DMA((len(kept),)),
        ],
        compiler_params=pltpu.CompilerParams(vmem_limit_bytes=56 << 20),
        name="warp_and_pack",
    )(*operands)


def place_kernel(parcel_ref, out_ref, slot_rows, spread_left, spread_right, corner_x_wide):
    f32, bf16 = jnp.float32, jnp.bfloat16
    slots = parcel_ref.shape[0]
    tracts, rows = out_ref.shape[0], PATCH // out_ref.shape[0]
    pitch = slots + 1

    for i in range(BLK):
        start = min(i * BLK, WIDTH - LANES)
        piece = parcel_ref[:, start : start + LANES].astype(f32)
        if start != i * BLK:
            piece = jnp.roll(piece, start - i * BLK, axis=1)
        slot_rows[pl.ds(i, slots, stride=BLK + 1), :] = piece
    tail = parcel_ref[:, WIDTH - LANES :].astype(f32)
    corner_x = tail[:, EXTRA + 1 : EXTRA + 2]
    corner_x_wide[...] = jnp.broadcast_to(corner_x, (slots, PATCH))
    by_slot = jnp.transpose(tail, (1, 0))
    corner_y = by_slot[EXTRA : EXTRA + 1, :]
    weight = by_slot[EXTRA + 2 : EXTRA + 3, :]

    shift = (
        lax.broadcasted_iota(jnp.int32, (BLK, PATCH), 1)
        - lax.broadcasted_iota(jnp.int32, (BLK, PATCH), 0)
    ).astype(f32)
    batch = 16
    for first in range(0, slots, batch):
        placed = []
        for s in range(first, first + batch):
            column = jnp.where(shift == corner_x_wide[s : s + 1, :], 1.0, 0.0).astype(bf16)
            block = slot_rows[(BLK + 1) * s : (BLK + 1) * s + BLK, :][:, :BLK].astype(bf16)
            placed.append(jnp.dot(block, column, preferred_element_type=f32))
        for s in range(first, first + batch):
            spread_left[pl.ds(s, BLK, stride=pitch), :] = placed[s - first][:, :LANES]
            spread_right[pl.ds(s, BLK, stride=pitch), :] = placed[s - first][:, LANES:]

    above = lax.broadcasted_iota(jnp.int32, (PATCH, slots), 0).astype(f32) - corner_y
    flux = jnp.zeros((PATCH, PATCH), f32)
    depth = 2
    for i in range(0, BLK, depth):
        row = jnp.concatenate(
            [jnp.where(above == float(i + n), weight, 0.0).astype(bf16) for n in range(depth)], axis=1
        )
        across = jnp.concatenate(
            [
                jnp.concatenate(
                    [half[pitch * (i + n) : pitch * (i + n) + slots, :] for n in range(depth)], axis=0
                )
                for half in (spread_left, spread_right)
            ],
            axis=1,
        ).astype(bf16)
        flux += jnp.dot(row, across, preferred_element_type=f32)
    beside = lax.broadcasted_iota(jnp.int32, (slots, PATCH), 1).astype(f32) - corner_x
    row_cover = jnp.where((above >= 0.0) & (above < float(BLK)), weight, 0.0).astype(bf16)
    column_cover = jnp.where((beside >= 0.0) & (beside < float(BLK)), 1.0, 0.0).astype(bf16)
    cover = jnp.dot(row_cover, column_cover, preferred_element_type=f32)
    for t in range(tracts):
        out_ref[t, :rows, :] = flux[rows * t : rows * (t + 1), :].astype(bf16)
        out_ref[t, rows:, :] = cover[rows * t : rows * (t + 1), :].astype(bf16)


def place(parcel, tracts):
    slots = parcel.shape[0]
    f32 = jnp.float32
    return pl.pallas_call(
        place_kernel,
        out_shape=jax.ShapeDtypeStruct((tracts, 2 * PATCH // tracts, PATCH), jnp.bfloat16),
        scratch_shapes=[
            pltpu.VMEM((slots * (BLK + 1), LANES), f32),
            pltpu.VMEM(((slots + 1) * BLK, LANES), f32),
            pltpu.VMEM(((slots + 1) * BLK, LANES), f32),
            pltpu.VMEM((slots, PATCH), f32),
        ],
        compiler_params=pltpu.CompilerParams(vmem_limit_bytes=24 << 20),
        name="place_in_patch",
    )(parcel)


def per_device(images, coefficients, orders, resample, weights, routes, offsets):
    visit_count = lax.axis_size("visit")
    tract_count = lax.axis_size("tract")
    capacity = 2
    slot_count = visit_count * capacity
    parcel = warp_and_pack(
        images[0],
        coefficients[0],
        orders,
        resample[0],
        weights,
        routes[0],
        offsets[0],
        slot_count,
    )
    parcel = lax.all_to_all(
        parcel.reshape(visit_count, capacity, WIDTH), "visit", split_axis=0, concat_axis=0, tiled=True
    ).reshape(slot_count, WIDTH)
    both = place(parcel, tract_count)
    both = lax.all_to_all(both, "tract", split_axis=0, concat_axis=0, tiled=True)
    sums = jnp.sum(both.astype(jnp.float32), axis=0)
    rows = PATCH // tract_count
    return (sums[None, :rows], sums[None, rows:])


def solution(mesh):
    in_specs = (
        P("tract", "visit", None),
        P("tract", "visit", None),
        P("tract", "visit"),
        P("tract", "visit", None),
        P("tract", "visit"),
        P("tract", "visit", None),
        P("tract", "visit", None, None),
    )
    out_specs = (P("visit", "tract", None), P("visit", "tract", None))
    return jax.shard_map(
        per_device, mesh=mesh, in_specs=in_specs, out_specs=out_specs, check_vma=False
    )
```

```python
import functools

import jax
import jax.numpy as jnp
import numpy as np
from jax import lax
from jax.experimental import pallas as pl
from jax.experimental.pallas import tpu as pltpu
from jax.sharding import PartitionSpec as P

KSIZE = 41
NBASIS = 16
NTERMS = 6
TOP = 2
BLK = 40
PATCH = 256
HALF = 20
BLKIN = 80
LANES = 128
WIDTH = 1664
EXTRA = 1600 % LANES

SIGMAS = (0.7, 1.5, 3.0, 2.0)
POWERS = (0, 0, 0, 1)
COLUMN_AT = (0, 40, 80, 128)


def constant_tables():
    difference = np.arange(BLKIN)[None, :] - np.arange(BLK)[:, None]
    inside = (difference >= 0) & (difference < KSIZE)
    shifted = (difference - HALF).astype(np.float32)
    taps = np.arange(KSIZE, dtype=np.float32) - np.float32(HALF)
    tables = []
    for sigma, power in zip(SIGMAS, POWERS):

        def profile(offset):
            value = np.exp(-offset * offset / np.float32(2.0 * sigma * sigma)).astype(np.float32)
            if power == 1:
                value = value * offset / np.float32(sigma)
            return value.astype(np.float32)

        total = np.sum(np.abs(profile(taps)), dtype=np.float32)
        tables.append(np.where(inside, profile(shifted) / total, np.float32(0.0)))
    held = np.zeros((4 * BLK + LANES, 2 * LANES), np.float32)
    held[: 4 * BLK, :BLKIN] = np.concatenate(tables, axis=0)
    for c, at in enumerate(COLUMN_AT):
        held[4 * BLK : 4 * BLK + BLKIN, at : at + BLK] = tables[c].T
    return jnp.asarray(held, jnp.bfloat16)


def warp_kernel(
    images_ref,
    coefficients_ref,
    orders_ref,
    resample_ref,
    weights_ref,
    routes_ref,
    offsets_ref,
    tables_ref,
    out_ref,
    image_rows,
    resample_rows,
    planes,
    warped_rows,
    flat,
    *held,
):
    f32, bf16 = jnp.float32, jnp.bfloat16
    *held, arrival = held
    sources = (
        images_ref,
        resample_ref,
        coefficients_ref,
        orders_ref,
        weights_ref,
        routes_ref,
        offsets_ref,
        tables_ref,
    )
    copies = [
        pltpu.make_async_copy(source, kept, arrival.at[number])
        for number, (source, kept) in enumerate(zip(sources, held, strict=True))
    ]
    for copy in copies:
        copy.start()
    (
        images_ref,
        resample_ref,
        coefficients_ref,
        orders_ref,
        weights_ref,
        routes_ref,
        offsets_ref,
        tables_ref,
    ) = held
    copies[0].wait()
    blocks = images_ref.shape[0]
    wide = 2 * LANES

    for x in range(BLKIN):
        start = min(x * BLKIN, BLKIN * BLKIN - LANES)
        piece = images_ref[:, start : start + LANES].astype(f32)
        if start != x * BLKIN:
            piece = jnp.roll(piece, start - x * BLKIN, axis=1)
        image_rows[pl.ds(x, blocks, stride=BLKIN + 1), :] = piece
    copies[1].wait()
    for copy in copies[2:]:
        copy.wait()
    for x in range(2 * BLK):
        start = min(x * BLK, 2 * BLK * BLK - LANES)
        piece = resample_ref[:, start : start + LANES].astype(f32)
        if start != x * BLK:
            piece = jnp.roll(piece, start - x * BLK, axis=1)
        resample_rows[pl.ds(x, blocks, stride=2 * BLK + 1), :] = piece

    terms = jnp.concatenate(
        [coefficients_ref[:, 4 * NTERMS * r : 4 * NTERMS * (r + 1)] for r in range(4)], axis=0
    )
    term_id = lax.broadcasted_iota(jnp.int32, (4 * NTERMS, wide), 0)
    lane = lax.broadcasted_iota(jnp.int32, (4 * NTERMS, wide), 1)
    column_kernel = sum((lane >= at).astype(jnp.int32) for at in COLUMN_AT[1:])
    spread = jnp.concatenate(
        [
            jnp.where(term_id == NTERMS * column_kernel + m, 1.0, 0.0).astype(bf16)
            for m in range(NTERMS)
        ],
        axis=1,
    )
    spread = jnp.dot(terms, spread, preferred_element_type=f32)
    lane = lax.broadcasted_iota(jnp.int32, (blocks, blocks), 1)
    sublane = lax.broadcasted_iota(jnp.int32, (blocks, blocks), 0)
    order = jnp.sum(
        jnp.where(lane == sublane, orders_ref[...].astype(f32), 0.0), axis=1, keepdims=True
    )
    order = jnp.concatenate([order] * 4, axis=0)
    first, second = order >= 1.0, order >= 2.0
    term = [spread[:, wide * m : wide * (m + 1)] for m in range(NTERMS)]
    term = (
        term[:1]
        + [jnp.where(first, t, 0.0) for t in term[1:3]]
        + [jnp.where(second, t, 0.0) for t in term[3:]]
    )
    lane = lax.broadcasted_iota(jnp.int32, (1, wide), 1)
    within = lane
    for at in COLUMN_AT[1:]:
        within = jnp.where(lane >= at, lane - at, within)
    across = (2.0 * within.astype(f32) + 1.0) / BLK - 1.0
    planes[:, :wide] = term[0] + across * (term[2] + across * term[5])
    planes[:, wide : 2 * wide] = term[1] + across * term[4]
    planes[:, 2 * wide :] = term[3]

    row_id = lax.broadcasted_iota(jnp.int32, (BLK, wide), 0).astype(f32)
    down = (2.0 * row_id + 1.0) / BLK - 1.0

    stacked = jnp.concatenate(
        [
            image_rows[(BLKIN + 1) * g : (BLKIN + 1) * g + BLKIN, :]
            for g in range(blocks)
        ],
        axis=1,
    ).astype(bf16)
    smooth = jnp.dot(tables_ref[: 4 * BLK, :BLKIN], stacked, preferred_element_type=f32).astype(bf16)
    responses = [
        jnp.dot(
            smooth[:, LANES * g : LANES * (g + 1)],
            tables_ref[4 * BLK :, :],
            preferred_element_type=f32,
        )
        for g in range(blocks)
    ]
    matched = []
    for g in range(blocks):
        total = jnp.zeros((BLK, wide), f32)
        for r in range(4):
            plane = planes[r * blocks + g : r * blocks + g + 1, :]
            weight = plane[:, :wide] + down * (
                plane[:, wide : 2 * wide] + down * plane[:, 2 * wide :]
            )
            total = total + weight * responses[g][BLK * r : BLK * (r + 1), :]
        low, high = total[:, :LANES], total[:, LANES:]
        folded = (
            low
            + high
            + pltpu.roll(low, LANES - BLK, axis=1)
            + pltpu.roll(low, LANES - 2 * BLK, axis=1)
        )
        matched.append(folded[:, :BLK].astype(bf16))
    halfway = [
        jnp.dot(
            resample_rows[(2 * BLK + 1) * g : (2 * BLK + 1) * g + BLK, :][:, :BLK].astype(bf16),
            matched[g],
            preferred_element_type=f32,
        ).astype(bf16)
        for g in range(blocks)
    ]
    warped = [
        lax.dot_general(
            halfway[g],
            resample_rows[(2 * BLK + 1) * g + BLK : (2 * BLK + 1) * (g + 1) - 1, :][:, :BLK].astype(bf16),
            (((1,), (1,)), ((), ())),
            preferred_element_type=f32,
        )
        for g in range(blocks)
    ]
    for g in range(blocks):
        warped_rows[(BLK + 1) * g : (BLK + 1) * g + BLK, 0:BLK] = warped[g]
    flat[:, 12 * LANES :] = jnp.zeros((blocks, LANES), f32)
    for i in range(BLK):
        flat[:, BLK * i : BLK * (i + 1)] = warped_rows[pl.ds(i, blocks, stride=BLK + 1), 0:BLK]
    pixels = flat[...].astype(bf16)

    slots, pairs = out_ref.shape[0] * out_ref.shape[1], TOP * blocks
    patch = jnp.concatenate([routes_ref[k : k + 1, :] for k in range(TOP)], axis=1)
    slot = lax.broadcasted_iota(jnp.int32, (slots, pairs), 0)
    hit = jnp.where(patch == slot // 2, 1.0, 0.0)
    before = lax.broadcasted_iota(jnp.int32, (pairs, pairs), 0)
    after = lax.broadcasted_iota(jnp.int32, (pairs, pairs), 1)
    rank = jnp.dot(
        hit.astype(bf16),
        jnp.where(before < after, 1.0, 0.0).astype(bf16),
        preferred_element_type=f32,
    )
    pick = jnp.where(rank == (slot % 2).astype(f32), hit, 0.0).astype(bf16)
    packed = jnp.dot(
        pick, jnp.concatenate([pixels] * TOP, axis=0), preferred_element_type=f32
    )
    column = lax.broadcasted_iota(jnp.int32, (LANES, pairs), 0) - EXTRA
    corner_y = jnp.concatenate([offsets_ref[k, 0:1, :] for k in range(TOP)], axis=1).astype(f32)
    corner_x = jnp.concatenate([offsets_ref[k, 1:2, :] for k in range(TOP)], axis=1).astype(f32)
    weight = jnp.concatenate([weights_ref[...].astype(f32)] * TOP, axis=1)
    extras = jnp.where(
        column == 0,
        corner_y,
        jnp.where(column == 1, corner_x, jnp.where(column == 2, weight, 0.0)),
    ).astype(bf16)
    tail = lax.dot_general(pick, extras, (((1,), (1,)), ((), ())), preferred_element_type=f32)
    packed = jnp.concatenate([packed[:, : 12 * LANES], packed[:, 12 * LANES :] + tail], axis=1)
    out_ref[...] = packed.astype(bf16).reshape(out_ref.shape)


def warp_and_pack(images, coefficients, orders, resample, weights, routes, offsets, slots):
    blocks = images.shape[0]
    f32 = jnp.float32
    operands = (
        images,
        coefficients,
        orders,
        resample,
        weights,
        jnp.transpose(routes, (1, 0)),
        jnp.transpose(offsets, (1, 2, 0)),
        constant_tables(),
    )
    kept = [operands[n] for n in (0, 3, 1, 2, 4, 5, 6, 7)]
    return pl.pallas_call(
        warp_kernel,
        out_shape=jax.ShapeDtypeStruct((slots // 2, 2, WIDTH), jnp.bfloat16),
        in_specs=[pl.BlockSpec(memory_space=pl.ANY)] * len(operands),
        scratch_shapes=[
            pltpu.VMEM((blocks * (BLKIN + 1), LANES), f32),
            pltpu.VMEM((blocks * (2 * BLK + 1), LANES), f32),
            pltpu.VMEM((blocks * 4, 3 * 2 * LANES), f32),
            pltpu.VMEM((blocks * (BLK + 1), LANES), f32),
            pltpu.VMEM((blocks, WIDTH), f32),
            *[pltpu.VMEM(array.shape, array.dtype) for array in kept],
            pltpu.SemaphoreType.DMA((len(kept),)),
        ],
        compiler_params=pltpu.CompilerParams(vmem_limit_bytes=56 << 20),
        name="warp_and_pack",
    )(*operands)


def place_kernel(parcel_ref, out_ref, slot_rows, spread_left, spread_right, corner_x_wide):
    f32, bf16 = jnp.float32, jnp.bfloat16
    slots = parcel_ref.shape[0]
    tracts, rows = out_ref.shape[0], PATCH // out_ref.shape[0]
    pitch = slots + 1

    for i in range(BLK):
        start = min(i * BLK, WIDTH - LANES)
        piece = parcel_ref[:, start : start + LANES].astype(f32)
        if start != i * BLK:
            piece = jnp.roll(piece, start - i * BLK, axis=1)
        slot_rows[pl.ds(i, slots, stride=BLK + 1), :] = piece
    tail = parcel_ref[:, WIDTH - LANES :].astype(f32)
    corner_x = tail[:, EXTRA + 1 : EXTRA + 2]
    corner_x_wide[...] = jnp.broadcast_to(corner_x, (slots, PATCH))
    by_slot = jnp.transpose(tail, (1, 0))
    corner_y = by_slot[EXTRA : EXTRA + 1, :]
    corner_x_row = by_slot[EXTRA + 1 : EXTRA + 2, :]
    weight = by_slot[EXTRA + 2 : EXTRA + 3, :]

    shift = (
        lax.broadcasted_iota(jnp.int32, (BLK, PATCH), 1)
        - lax.broadcasted_iota(jnp.int32, (BLK, PATCH), 0)
    ).astype(f32)
    batch = 16
    for first in range(0, slots, batch):
        placed = []
        for s in range(first, first + batch):
            column = jnp.where(shift == corner_x_wide[s : s + 1, :], 1.0, 0.0).astype(bf16)
            block = slot_rows[(BLK + 1) * s : (BLK + 1) * s + BLK, :][:, :BLK].astype(bf16)
            placed.append(jnp.dot(block, column, preferred_element_type=f32))
        for s in range(first, first + batch):
            spread_left[pl.ds(s, BLK, stride=pitch), :] = placed[s - first][:, :LANES]
            spread_right[pl.ds(s, BLK, stride=pitch), :] = placed[s - first][:, LANES:]

    above = lax.broadcasted_iota(jnp.int32, (PATCH, slots), 0).astype(f32) - corner_y
    flux = jnp.zeros((PATCH, PATCH), f32)
    depth = 2
    for i in range(0, BLK, depth):
        row = jnp.concatenate(
            [jnp.where(above == float(i + n), weight, 0.0).astype(bf16) for n in range(depth)], axis=1
        )
        across = jnp.concatenate(
            [
                jnp.concatenate(
                    [half[pitch * (i + n) : pitch * (i + n) + slots, :] for n in range(depth)], axis=0
                )
                for half in (spread_left, spread_right)
            ],
            axis=1,
        ).astype(bf16)
        flux += jnp.dot(row, across, preferred_element_type=f32)
    blank = jnp.zeros((6, PATCH), f32)
    for t in range(tracts):
        corners = jnp.concatenate([corner_y - float(rows * t), corner_x_row], axis=1)
        weights = jnp.concatenate([weight, jnp.zeros_like(weight)], axis=1)
        parts = [flux[rows * t : rows * (t + 1), :], corners, weights, blank]
        out_ref[t] = jnp.concatenate(parts, axis=0).astype(bf16)


def place(parcel, tracts):
    slots = parcel.shape[0]
    f32 = jnp.float32
    return pl.pallas_call(
        place_kernel,
        out_shape=jax.ShapeDtypeStruct((tracts, PATCH // tracts + 8, PATCH), jnp.bfloat16),
        scratch_shapes=[
            pltpu.VMEM((slots * (BLK + 1), LANES), f32),
            pltpu.VMEM(((slots + 1) * BLK, LANES), f32),
            pltpu.VMEM(((slots + 1) * BLK, LANES), f32),
            pltpu.VMEM((slots, PATCH), f32),
        ],
        compiler_params=pltpu.CompilerParams(vmem_limit_bytes=24 << 20),
        name="place_in_patch",
    )(parcel)


def finish_kernel(parts_ref, flux_ref, cover_ref):
    f32, bf16 = jnp.float32, jnp.bfloat16
    rows, slots = flux_ref.shape[0], PATCH // 2
    y = lax.broadcasted_iota(jnp.int32, (rows, slots), 0).astype(f32)
    x = lax.broadcasted_iota(jnp.int32, (PATCH, slots), 0).astype(f32)
    flux = jnp.zeros((rows, PATCH), f32)
    cover = jnp.zeros((rows, PATCH), f32)
    for t in range(parts_ref.shape[0]):
        part = parts_ref[t].astype(f32)
        flux += part[:rows, :]
        extras = part[rows:, :]
        down = y - extras[0:1, :slots]
        across = x - extras[0:1, slots:]
        row = jnp.where((down >= 0.0) & (down < float(BLK)), extras[1:2, :slots], 0.0)
        column = jnp.where((across >= 0.0) & (across < float(BLK)), 1.0, 0.0)
        cover += lax.dot_general(
            row.astype(bf16),
            column.astype(bf16),
            (((1,), (1,)), ((), ())),
            preferred_element_type=f32,
        )
    flux_ref[...] = flux
    cover_ref[...] = cover


def finish(parts, tracts):
    out = jax.ShapeDtypeStruct((PATCH // tracts, PATCH), jnp.float32)
    return pl.pallas_call(
        finish_kernel,
        out_shape=(out, out),
        compiler_params=pltpu.CompilerParams(vmem_limit_bytes=16 << 20),
        name="finish",
    )(parts)


def per_device(images, coefficients, orders, resample, weights, routes, offsets):
    visit_count = lax.axis_size("visit")
    tract_count = lax.axis_size("tract")
    capacity = 2
    slot_count = visit_count * capacity
    parcel = warp_and_pack(
        images[0],
        coefficients[0],
        orders,
        resample[0],
        weights,
        routes[0],
        offsets[0],
        slot_count,
    )
    parcel = lax.all_to_all(
        parcel, "visit", split_axis=0, concat_axis=0, tiled=True
    ).reshape(slot_count, WIDTH)
    parts = place(parcel, tract_count)
    parts = lax.all_to_all(parts, "tract", split_axis=0, concat_axis=0, tiled=True)
    flux, cover = finish(parts, tract_count)
    return (flux[None], cover[None])


def solution(mesh):
    in_specs = (
        P("tract", "visit", None),
        P("tract", "visit", None),
        P("tract", "visit"),
        P("tract", "visit", None),
        P("tract", "visit"),
        P("tract", "visit", None),
        P("tract", "visit", None, None),
    )
    out_specs = (P("visit", "tract", None), P("visit", "tract", None))
    return jax.shard_map(
        per_device, mesh=mesh, in_specs=in_specs, out_specs=out_specs, check_vma=False
    )
```

```python
import functools

import jax
import jax.numpy as jnp
import numpy as np
from jax import lax
from jax.experimental import pallas as pl
from jax.experimental.pallas import tpu as pltpu
from jax.sharding import PartitionSpec as P

KSIZE = 41
NBASIS = 16
NTERMS = 6
TOP = 2
BLK = 40
PATCH = 256
HALF = 20
BLKIN = 80
LANES = 128
WIDTH = 1664
EXTRA = 1600 % LANES

SIGMAS = (0.7, 1.5, 3.0, 2.0)
POWERS = (0, 0, 0, 1)
COLUMN_AT = (0, 40, 80, 128)


DEEP = 16
START = (2, 8)


def visit_order(count):
    wide = count // DEEP
    return [
        (x + START[0]) % wide * DEEP + (z + START[1]) % DEEP for x in range(wide) for z in range(DEEP)
    ]


def constant_tables():
    difference = np.arange(BLKIN)[None, :] - np.arange(BLK)[:, None]
    inside = (difference >= 0) & (difference < KSIZE)
    shifted = (difference - HALF).astype(np.float32)
    taps = np.arange(KSIZE, dtype=np.float32) - np.float32(HALF)
    tables = []
    for sigma, power in zip(SIGMAS, POWERS):

        def profile(offset):
            value = np.exp(-offset * offset / np.float32(2.0 * sigma * sigma)).astype(np.float32)
            if power == 1:
                value = value * offset / np.float32(sigma)
            return value.astype(np.float32)

        total = np.sum(np.abs(profile(taps)), dtype=np.float32)
        tables.append(np.where(inside, profile(shifted) / total, np.float32(0.0)))
    held = np.zeros((4 * BLK + LANES, 2 * LANES), np.float32)
    held[: 4 * BLK, :BLKIN] = np.concatenate(tables, axis=0)
    for c, at in enumerate(COLUMN_AT):
        held[4 * BLK : 4 * BLK + BLKIN, at : at + BLK] = tables[c].T
    return jnp.asarray(held, jnp.bfloat16)


def warp_kernel(
    images_ref,
    coefficients_ref,
    orders_ref,
    resample_ref,
    weights_ref,
    routes_ref,
    offsets_ref,
    tables_ref,
    out_ref,
    image_rows,
    resample_rows,
    planes,
    warped_rows,
    flat,
    *held,
):
    f32, bf16 = jnp.float32, jnp.bfloat16
    *held, arrival = held
    sources = (
        images_ref,
        resample_ref,
        coefficients_ref,
        orders_ref,
        weights_ref,
        routes_ref,
        offsets_ref,
        tables_ref,
    )
    copies = [
        pltpu.make_async_copy(source, kept, arrival.at[number])
        for number, (source, kept) in enumerate(zip(sources, held, strict=True))
    ]
    for copy in copies:
        copy.start()
    (
        images_ref,
        resample_ref,
        coefficients_ref,
        orders_ref,
        weights_ref,
        routes_ref,
        offsets_ref,
        tables_ref,
    ) = held
    copies[0].wait()
    blocks = images_ref.shape[0]
    wide = 2 * LANES

    for x in range(BLKIN):
        start = min(x * BLKIN, BLKIN * BLKIN - LANES)
        piece = images_ref[:, start : start + LANES].astype(f32)
        if start != x * BLKIN:
            piece = jnp.roll(piece, start - x * BLKIN, axis=1)
        image_rows[pl.ds(x, blocks, stride=BLKIN + 1), :] = piece
    copies[1].wait()
    for copy in copies[2:]:
        copy.wait()
    for x in range(2 * BLK):
        start = min(x * BLK, 2 * BLK * BLK - LANES)
        piece = resample_ref[:, start : start + LANES].astype(f32)
        if start != x * BLK:
            piece = jnp.roll(piece, start - x * BLK, axis=1)
        resample_rows[pl.ds(x, blocks, stride=2 * BLK + 1), :] = piece

    terms = jnp.concatenate(
        [coefficients_ref[:, 4 * NTERMS * r : 4 * NTERMS * (r + 1)] for r in range(4)], axis=0
    )
    term_id = lax.broadcasted_iota(jnp.int32, (4 * NTERMS, wide), 0)
    lane = lax.broadcasted_iota(jnp.int32, (4 * NTERMS, wide), 1)
    column_kernel = sum((lane >= at).astype(jnp.int32) for at in COLUMN_AT[1:])
    spread = jnp.concatenate(
        [
            jnp.where(term_id == NTERMS * column_kernel + m, 1.0, 0.0).astype(bf16)
            for m in range(NTERMS)
        ],
        axis=1,
    )
    spread = jnp.dot(terms, spread, preferred_element_type=f32)
    lane = lax.broadcasted_iota(jnp.int32, (blocks, blocks), 1)
    sublane = lax.broadcasted_iota(jnp.int32, (blocks, blocks), 0)
    order = jnp.sum(
        jnp.where(lane == sublane, orders_ref[...].astype(f32), 0.0), axis=1, keepdims=True
    )
    order = jnp.concatenate([order] * 4, axis=0)
    first, second = order >= 1.0, order >= 2.0
    term = [spread[:, wide * m : wide * (m + 1)] for m in range(NTERMS)]
    term = (
        term[:1]
        + [jnp.where(first, t, 0.0) for t in term[1:3]]
        + [jnp.where(second, t, 0.0) for t in term[3:]]
    )
    lane = lax.broadcasted_iota(jnp.int32, (1, wide), 1)
    within = lane
    for at in COLUMN_AT[1:]:
        within = jnp.where(lane >= at, lane - at, within)
    across = (2.0 * within.astype(f32) + 1.0) / BLK - 1.0
    planes[:, :wide] = term[0] + across * (term[2] + across * term[5])
    planes[:, wide : 2 * wide] = term[1] + across * term[4]
    planes[:, 2 * wide :] = term[3]

    row_id = lax.broadcasted_iota(jnp.int32, (BLK, wide), 0).astype(f32)
    down = (2.0 * row_id + 1.0) / BLK - 1.0

    stacked = jnp.concatenate(
        [
            image_rows[(BLKIN + 1) * g : (BLKIN + 1) * g + BLKIN, :]
            for g in range(blocks)
        ],
        axis=1,
    ).astype(bf16)
    smooth = jnp.dot(tables_ref[: 4 * BLK, :BLKIN], stacked, preferred_element_type=f32).astype(bf16)
    responses = [
        jnp.dot(
            smooth[:, LANES * g : LANES * (g + 1)],
            tables_ref[4 * BLK :, :],
            preferred_element_type=f32,
        )
        for g in range(blocks)
    ]
    matched = []
    for g in range(blocks):
        total = jnp.zeros((BLK, wide), f32)
        for r in range(4):
            plane = planes[r * blocks + g : r * blocks + g + 1, :]
            weight = plane[:, :wide] + down * (
                plane[:, wide : 2 * wide] + down * plane[:, 2 * wide :]
            )
            total = total + weight * responses[g][BLK * r : BLK * (r + 1), :]
        low, high = total[:, :LANES], total[:, LANES:]
        folded = (
            low
            + high
            + pltpu.roll(low, LANES - BLK, axis=1)
            + pltpu.roll(low, LANES - 2 * BLK, axis=1)
        )
        matched.append(folded[:, :BLK].astype(bf16))
    halfway = [
        jnp.dot(
            resample_rows[(2 * BLK + 1) * g : (2 * BLK + 1) * g + BLK, :][:, :BLK].astype(bf16),
            matched[g],
            preferred_element_type=f32,
        ).astype(bf16)
        for g in range(blocks)
    ]
    warped = [
        lax.dot_general(
            halfway[g],
            resample_rows[(2 * BLK + 1) * g + BLK : (2 * BLK + 1) * (g + 1) - 1, :][:, :BLK].astype(bf16),
            (((1,), (1,)), ((), ())),
            preferred_element_type=f32,
        )
        for g in range(blocks)
    ]
    for g in range(blocks):
        warped_rows[(BLK + 1) * g : (BLK + 1) * g + BLK, 0:BLK] = warped[g]
    flat[:, 12 * LANES :] = jnp.zeros((blocks, LANES), f32)
    for i in range(BLK):
        flat[:, BLK * i : BLK * (i + 1)] = warped_rows[pl.ds(i, blocks, stride=BLK + 1), 0:BLK]
    pixels = flat[...].astype(bf16)

    slots, pairs = out_ref.shape[0] * out_ref.shape[1], TOP * blocks
    patch = jnp.concatenate([routes_ref[k : k + 1, :] for k in range(TOP)], axis=1)
    slot = lax.broadcasted_iota(jnp.int32, (slots, pairs), 0)
    place = slot // 2
    member = ((place + DEEP * START[0]) & (-DEEP & (slots // 2 - 1))) | (
        (place + START[1]) & (DEEP - 1)
    )
    hit = jnp.where(patch == member, 1.0, 0.0)
    before = lax.broadcasted_iota(jnp.int32, (pairs, pairs), 0)
    after = lax.broadcasted_iota(jnp.int32, (pairs, pairs), 1)
    rank = jnp.dot(
        hit.astype(bf16),
        jnp.where(before < after, 1.0, 0.0).astype(bf16),
        preferred_element_type=f32,
    )
    pick = jnp.where(rank == (slot % 2).astype(f32), hit, 0.0).astype(bf16)
    packed = jnp.dot(
        pick, jnp.concatenate([pixels] * TOP, axis=0), preferred_element_type=f32
    )
    column = lax.broadcasted_iota(jnp.int32, (LANES, pairs), 0) - EXTRA
    corner_y = jnp.concatenate([offsets_ref[k, 0:1, :] for k in range(TOP)], axis=1).astype(f32)
    corner_x = jnp.concatenate([offsets_ref[k, 1:2, :] for k in range(TOP)], axis=1).astype(f32)
    weight = jnp.concatenate([weights_ref[...].astype(f32)] * TOP, axis=1)
    extras = jnp.where(
        column == 0,
        corner_y,
        jnp.where(column == 1, corner_x, jnp.where(column == 2, weight, 0.0)),
    ).astype(bf16)
    tail = lax.dot_general(pick, extras, (((1,), (1,)), ((), ())), preferred_element_type=f32)
    packed = jnp.concatenate([packed[:, : 12 * LANES], packed[:, 12 * LANES :] + tail], axis=1)
    out_ref[...] = packed.astype(bf16).reshape(out_ref.shape)


def warp_and_pack(images, coefficients, orders, resample, weights, routes, offsets, slots):
    blocks = images.shape[0]
    f32 = jnp.float32
    operands = (
        images,
        coefficients,
        orders,
        resample,
        weights,
        jnp.transpose(routes, (1, 0)),
        jnp.transpose(offsets, (1, 2, 0)),
        constant_tables(),
    )
    kept = [operands[n] for n in (0, 3, 1, 2, 4, 5, 6, 7)]
    return pl.pallas_call(
        warp_kernel,
        out_shape=jax.ShapeDtypeStruct((slots // 2, 2, WIDTH), jnp.bfloat16),
        in_specs=[pl.BlockSpec(memory_space=pl.ANY)] * len(operands),
        scratch_shapes=[
            pltpu.VMEM((blocks * (BLKIN + 1), LANES), f32),
            pltpu.VMEM((blocks * (2 * BLK + 1), LANES), f32),
            pltpu.VMEM((blocks * 4, 3 * 2 * LANES), f32),
            pltpu.VMEM((blocks * (BLK + 1), LANES), f32),
            pltpu.VMEM((blocks, WIDTH), f32),
            *[pltpu.VMEM(array.shape, array.dtype) for array in kept],
            pltpu.SemaphoreType.DMA((len(kept),)),
        ],
        compiler_params=pltpu.CompilerParams(vmem_limit_bytes=32 << 20),
        name="warp_and_pack",
    )(*[pltpu.with_memory_space_constraint(array, pltpu.HBM) for array in operands])


def place_kernel(parcel_ref, out_ref, slot_rows, spread_left, spread_right, corner_x_wide):
    f32, bf16 = jnp.float32, jnp.bfloat16
    slots = parcel_ref.shape[0]
    tracts, rows = out_ref.shape[0], PATCH // out_ref.shape[0]
    pitch = slots + 1

    for i in range(BLK):
        start = min(i * BLK, WIDTH - LANES)
        piece = parcel_ref[:, start : start + LANES].astype(f32)
        if start != i * BLK:
            piece = jnp.roll(piece, start - i * BLK, axis=1)
        slot_rows[pl.ds(i, slots, stride=BLK + 1), :] = piece
    tail = parcel_ref[:, WIDTH - LANES :].astype(f32)
    corner_x = tail[:, EXTRA + 1 : EXTRA + 2]
    corner_x_wide[...] = jnp.broadcast_to(corner_x, (slots, PATCH))
    by_slot = jnp.transpose(tail, (1, 0))
    corner_y = by_slot[EXTRA : EXTRA + 1, :]
    corner_x_row = by_slot[EXTRA + 1 : EXTRA + 2, :]
    weight = by_slot[EXTRA + 2 : EXTRA + 3, :]

    shift = (
        lax.broadcasted_iota(jnp.int32, (BLK, PATCH), 1)
        - lax.broadcasted_iota(jnp.int32, (BLK, PATCH), 0)
    ).astype(f32)
    batch = 16
    for first in range(0, slots, batch):
        placed = []
        for s in range(first, first + batch):
            column = jnp.where(shift == corner_x_wide[s : s + 1, :], 1.0, 0.0).astype(bf16)
            block = slot_rows[(BLK + 1) * s : (BLK + 1) * s + BLK, :][:, :BLK].astype(bf16)
            placed.append(jnp.dot(block, column, preferred_element_type=f32))
        for s in range(first, first + batch):
            spread_left[pl.ds(s, BLK, stride=pitch), :] = placed[s - first][:, :LANES]
            spread_right[pl.ds(s, BLK, stride=pitch), :] = placed[s - first][:, LANES:]

    above = lax.broadcasted_iota(jnp.int32, (PATCH, slots), 0).astype(f32) - corner_y
    flux = jnp.zeros((PATCH, PATCH), f32)
    depth = 2
    for i in range(0, BLK, depth):
        row = jnp.concatenate(
            [jnp.where(above == float(i + n), weight, 0.0).astype(bf16) for n in range(depth)], axis=1
        )
        across = jnp.concatenate(
            [
                jnp.concatenate(
                    [half[pitch * (i + n) : pitch * (i + n) + slots, :] for n in range(depth)], axis=0
                )
                for half in (spread_left, spread_right)
            ],
            axis=1,
        ).astype(bf16)
        flux += jnp.dot(row, across, preferred_element_type=f32)
    blank = jnp.zeros((6, PATCH), f32)
    for t in range(tracts):
        corners = jnp.concatenate([corner_y - float(rows * t), corner_x_row], axis=1)
        weights = jnp.concatenate([weight, jnp.zeros_like(weight)], axis=1)
        parts = [flux[rows * t : rows * (t + 1), :], corners, weights, blank]
        out_ref[t] = jnp.concatenate(parts, axis=0).astype(bf16)


def place(parcel, tracts):
    slots = parcel.shape[0]
    f32 = jnp.float32
    return pl.pallas_call(
        place_kernel,
        out_shape=jax.ShapeDtypeStruct((tracts, PATCH // tracts + 8, PATCH), jnp.bfloat16),
        scratch_shapes=[
            pltpu.VMEM((slots * (BLK + 1), LANES), f32),
            pltpu.VMEM(((slots + 1) * BLK, LANES), f32),
            pltpu.VMEM(((slots + 1) * BLK, LANES), f32),
            pltpu.VMEM((slots, PATCH), f32),
        ],
        compiler_params=pltpu.CompilerParams(vmem_limit_bytes=24 << 20),
        name="place_in_patch",
    )(parcel)


def finish_kernel(parts_ref, flux_ref, cover_ref):
    f32, bf16 = jnp.float32, jnp.bfloat16
    rows, slots = flux_ref.shape[0], PATCH // 2
    y = lax.broadcasted_iota(jnp.int32, (rows, slots), 0).astype(f32)
    x = lax.broadcasted_iota(jnp.int32, (PATCH, slots), 0).astype(f32)
    flux = jnp.zeros((rows, PATCH), f32)
    cover = jnp.zeros((rows, PATCH), f32)
    for t in range(parts_ref.shape[0]):
        part = parts_ref[t].astype(f32)
        flux += part[:rows, :]
        extras = part[rows:, :]
        down = y - extras[0:1, :slots]
        across = x - extras[0:1, slots:]
        row = jnp.where((down >= 0.0) & (down < float(BLK)), extras[1:2, :slots], 0.0)
        column = jnp.where((across >= 0.0) & (across < float(BLK)), 1.0, 0.0)
        cover += lax.dot_general(
            row.astype(bf16),
            column.astype(bf16),
            (((1,), (1,)), ((), ())),
            preferred_element_type=f32,
        )
    flux_ref[...] = flux
    cover_ref[...] = cover


def finish(parts, tracts):
    out = jax.ShapeDtypeStruct((PATCH // tracts, PATCH), jnp.float32)
    return pl.pallas_call(
        finish_kernel,
        out_shape=(out, out),
        compiler_params=pltpu.CompilerParams(vmem_limit_bytes=16 << 20),
        name="finish",
    )(parts)


def per_device(images, coefficients, orders, resample, weights, routes, offsets):
    visit_count = lax.axis_size("visit")
    tract_count = lax.axis_size("tract")
    capacity = 2
    slot_count = visit_count * capacity
    parcel = warp_and_pack(
        images[0],
        coefficients[0],
        orders,
        resample[0],
        weights,
        routes[0],
        offsets[0],
        slot_count,
    )
    parcel = lax.all_to_all(
        parcel,
        "visit",
        split_axis=0,
        concat_axis=0,
        tiled=True,
        axis_index_groups=[visit_order(visit_count)],
    ).reshape(slot_count, WIDTH)
    parts = place(parcel, tract_count)
    parts = lax.all_to_all(parts, "tract", split_axis=0, concat_axis=0, tiled=True)
    flux, cover = finish(parts, tract_count)
    return (flux[None], cover[None])


def solution(mesh):
    in_specs = (
        P("tract", "visit", None),
        P("tract", "visit", None),
        P("tract", "visit"),
        P("tract", "visit", None),
        P("tract", "visit"),
        P("tract", "visit", None),
        P("tract", "visit", None, None),
    )
    out_specs = (P("visit", "tract", None), P("visit", "tract", None))
    return jax.shard_map(
        per_device, mesh=mesh, in_specs=in_specs, out_specs=out_specs, check_vma=False
    )
```

```python
import functools

import jax
import jax.numpy as jnp
import numpy as np
from jax import lax
from jax.experimental import pallas as pl
from jax.experimental.pallas import tpu as pltpu
from jax.sharding import PartitionSpec as P

KSIZE = 41
NBASIS = 16
NTERMS = 6
TOP = 2
BLK = 40
PATCH = 256
HALF = 20
BLKIN = 80
LANES = 128
WIDTH = 1664
EXTRA = 1600 % LANES

SIGMAS = (0.7, 1.5, 3.0, 2.0)
POWERS = (0, 0, 0, 1)
COLUMN_AT = (0, 40, 80, 128)


DEEP = 16
START = (2, 8)
FIRST = 5


def visit_order(count):
    wide = count // DEEP
    return [
        (x + START[0]) % wide * DEEP + (z + START[1]) % DEEP for x in range(wide) for z in range(DEEP)
    ]


def tract_order(count):
    return [(t + FIRST) % count for t in range(count)]


def constant_tables():
    difference = np.arange(BLKIN)[None, :] - np.arange(BLK)[:, None]
    inside = (difference >= 0) & (difference < KSIZE)
    shifted = (difference - HALF).astype(np.float32)
    taps = np.arange(KSIZE, dtype=np.float32) - np.float32(HALF)
    tables = []
    for sigma, power in zip(SIGMAS, POWERS):

        def profile(offset):
            value = np.exp(-offset * offset / np.float32(2.0 * sigma * sigma)).astype(np.float32)
            if power == 1:
                value = value * offset / np.float32(sigma)
            return value.astype(np.float32)

        total = np.sum(np.abs(profile(taps)), dtype=np.float32)
        tables.append(np.where(inside, profile(shifted) / total, np.float32(0.0)))
    held = np.zeros((4 * BLK + LANES, 2 * LANES), np.float32)
    held[: 4 * BLK, :BLKIN] = np.concatenate(tables, axis=0)
    for c, at in enumerate(COLUMN_AT):
        held[4 * BLK : 4 * BLK + BLKIN, at : at + BLK] = tables[c].T
    return jnp.asarray(held, jnp.bfloat16)


def warp_kernel(
    images_ref,
    coefficients_ref,
    orders_ref,
    resample_ref,
    weights_ref,
    routes_ref,
    offsets_ref,
    tables_ref,
    out_ref,
    image_rows,
    resample_rows,
    planes,
    warped_rows,
    flat,
    *held,
):
    f32, bf16 = jnp.float32, jnp.bfloat16
    *held, arrival = held
    sources = (
        images_ref,
        resample_ref,
        coefficients_ref,
        orders_ref,
        weights_ref,
        routes_ref,
        offsets_ref,
        tables_ref,
    )
    copies = [
        pltpu.make_async_copy(source, kept, arrival.at[number])
        for number, (source, kept) in enumerate(zip(sources, held, strict=True))
    ]
    for copy in copies:
        copy.start()
    (
        images_ref,
        resample_ref,
        coefficients_ref,
        orders_ref,
        weights_ref,
        routes_ref,
        offsets_ref,
        tables_ref,
    ) = held
    copies[0].wait()
    blocks = images_ref.shape[0]
    wide = 2 * LANES

    for x in range(BLKIN):
        start = min(x * BLKIN, BLKIN * BLKIN - LANES)
        piece = images_ref[:, start : start + LANES].astype(f32)
        if start != x * BLKIN:
            piece = jnp.roll(piece, start - x * BLKIN, axis=1)
        image_rows[pl.ds(x, blocks, stride=BLKIN + 1), :] = piece
    copies[1].wait()
    for copy in copies[2:]:
        copy.wait()
    for x in range(2 * BLK):
        start = min(x * BLK, 2 * BLK * BLK - LANES)
        piece = resample_ref[:, start : start + LANES].astype(f32)
        if start != x * BLK:
            piece = jnp.roll(piece, start - x * BLK, axis=1)
        resample_rows[pl.ds(x, blocks, stride=2 * BLK + 1), :] = piece

    terms = jnp.concatenate(
        [coefficients_ref[:, 4 * NTERMS * r : 4 * NTERMS * (r + 1)] for r in range(4)], axis=0
    )
    term_id = lax.broadcasted_iota(jnp.int32, (4 * NTERMS, wide), 0)
    lane = lax.broadcasted_iota(jnp.int32, (4 * NTERMS, wide), 1)
    column_kernel = sum((lane >= at).astype(jnp.int32) for at in COLUMN_AT[1:])
    spread = jnp.concatenate(
        [
            jnp.where(term_id == NTERMS * column_kernel + m, 1.0, 0.0).astype(bf16)
            for m in range(NTERMS)
        ],
        axis=1,
    )
    spread = jnp.dot(terms, spread, preferred_element_type=f32)
    lane = lax.broadcasted_iota(jnp.int32, (blocks, blocks), 1)
    sublane = lax.broadcasted_iota(jnp.int32, (blocks, blocks), 0)
    order = jnp.sum(
        jnp.where(lane == sublane, orders_ref[...].astype(f32), 0.0), axis=1, keepdims=True
    )
    order = jnp.concatenate([order] * 4, axis=0)
    first, second = order >= 1.0, order >= 2.0
    term = [spread[:, wide * m : wide * (m + 1)] for m in range(NTERMS)]
    term = (
        term[:1]
        + [jnp.where(first, t, 0.0) for t in term[1:3]]
        + [jnp.where(second, t, 0.0) for t in term[3:]]
    )
    lane = lax.broadcasted_iota(jnp.int32, (1, wide), 1)
    within = lane
    for at in COLUMN_AT[1:]:
        within = jnp.where(lane >= at, lane - at, within)
    across = (2.0 * within.astype(f32) + 1.0) / BLK - 1.0
    planes[:, :wide] = term[0] + across * (term[2] + across * term[5])
    planes[:, wide : 2 * wide] = term[1] + across * term[4]
    planes[:, 2 * wide :] = term[3]

    row_id = lax.broadcasted_iota(jnp.int32, (BLK, wide), 0).astype(f32)
    down = (2.0 * row_id + 1.0) / BLK - 1.0

    stacked = jnp.concatenate(
        [
            image_rows[(BLKIN + 1) * g : (BLKIN + 1) * g + BLKIN, :]
            for g in range(blocks)
        ],
        axis=1,
    ).astype(bf16)
    smooth = jnp.dot(tables_ref[: 4 * BLK, :BLKIN], stacked, preferred_element_type=f32).astype(bf16)
    responses = [
        jnp.dot(
            smooth[:, LANES * g : LANES * (g + 1)],
            tables_ref[4 * BLK :, :],
            preferred_element_type=f32,
        )
        for g in range(blocks)
    ]
    matched = []
    for g in range(blocks):
        total = jnp.zeros((BLK, wide), f32)
        for r in range(4):
            plane = planes[r * blocks + g : r * blocks + g + 1, :]
            weight = plane[:, :wide] + down * (
                plane[:, wide : 2 * wide] + down * plane[:, 2 * wide :]
            )
            total = total + weight * responses[g][BLK * r : BLK * (r + 1), :]
        low, high = total[:, :LANES], total[:, LANES:]
        folded = (
            low
            + high
            + pltpu.roll(low, LANES - BLK, axis=1)
            + pltpu.roll(low, LANES - 2 * BLK, axis=1)
        )
        matched.append(folded[:, :BLK].astype(bf16))
    halfway = [
        jnp.dot(
            resample_rows[(2 * BLK + 1) * g : (2 * BLK + 1) * g + BLK, :][:, :BLK].astype(bf16),
            matched[g],
            preferred_element_type=f32,
        ).astype(bf16)
        for g in range(blocks)
    ]
    warped = [
        lax.dot_general(
            halfway[g],
            resample_rows[(2 * BLK + 1) * g + BLK : (2 * BLK + 1) * (g + 1) - 1, :][:, :BLK].astype(bf16),
            (((1,), (1,)), ((), ())),
            preferred_element_type=f32,
        )
        for g in range(blocks)
    ]
    for g in range(blocks):
        warped_rows[(BLK + 1) * g : (BLK + 1) * g + BLK, 0:BLK] = warped[g]
    flat[:, 12 * LANES :] = jnp.zeros((blocks, LANES), f32)
    for i in range(BLK):
        flat[:, BLK * i : BLK * (i + 1)] = warped_rows[pl.ds(i, blocks, stride=BLK + 1), 0:BLK]
    pixels = flat[...].astype(bf16)

    slots, pairs = out_ref.shape[0] * out_ref.shape[1], TOP * blocks
    patch = jnp.concatenate([routes_ref[k : k + 1, :] for k in range(TOP)], axis=1)
    slot = lax.broadcasted_iota(jnp.int32, (slots, pairs), 0)
    place = slot // 2
    member = ((place + DEEP * START[0]) & (-DEEP & (slots // 2 - 1))) | (
        (place + START[1]) & (DEEP - 1)
    )
    hit = jnp.where(patch == member, 1.0, 0.0)
    before = lax.broadcasted_iota(jnp.int32, (pairs, pairs), 0)
    after = lax.broadcasted_iota(jnp.int32, (pairs, pairs), 1)
    rank = jnp.dot(
        hit.astype(bf16),
        jnp.where(before < after, 1.0, 0.0).astype(bf16),
        preferred_element_type=f32,
    )
    pick = jnp.where(rank == (slot % 2).astype(f32), hit, 0.0).astype(bf16)
    packed = jnp.dot(
        pick, jnp.concatenate([pixels] * TOP, axis=0), preferred_element_type=f32
    )
    column = lax.broadcasted_iota(jnp.int32, (LANES, pairs), 0) - EXTRA
    corner_y = jnp.concatenate([offsets_ref[k, 0:1, :] for k in range(TOP)], axis=1).astype(f32)
    corner_x = jnp.concatenate([offsets_ref[k, 1:2, :] for k in range(TOP)], axis=1).astype(f32)
    weight = jnp.concatenate([weights_ref[...].astype(f32)] * TOP, axis=1)
    extras = jnp.where(
        column == 0,
        corner_y,
        jnp.where(column == 1, corner_x, jnp.where(column == 2, weight, 0.0)),
    ).astype(bf16)
    tail = lax.dot_general(pick, extras, (((1,), (1,)), ((), ())), preferred_element_type=f32)
    packed = jnp.concatenate([packed[:, : 12 * LANES], packed[:, 12 * LANES :] + tail], axis=1)
    out_ref[...] = packed.astype(bf16).reshape(out_ref.shape)


def warp_and_pack(images, coefficients, orders, resample, weights, routes, offsets, slots):
    blocks = images.shape[0]
    f32 = jnp.float32
    operands = (
        images,
        coefficients,
        orders,
        resample,
        weights,
        jnp.transpose(routes, (1, 0)),
        jnp.transpose(offsets, (1, 2, 0)),
        constant_tables(),
    )
    kept = [operands[n] for n in (0, 3, 1, 2, 4, 5, 6, 7)]
    return pl.pallas_call(
        warp_kernel,
        out_shape=jax.ShapeDtypeStruct((slots // 2, 2, WIDTH), jnp.bfloat16),
        in_specs=[pl.BlockSpec(memory_space=pl.ANY)] * len(operands),
        scratch_shapes=[
            pltpu.VMEM((blocks * (BLKIN + 1), LANES), f32),
            pltpu.VMEM((blocks * (2 * BLK + 1), LANES), f32),
            pltpu.VMEM((blocks * 4, 3 * 2 * LANES), f32),
            pltpu.VMEM((blocks * (BLK + 1), LANES), f32),
            pltpu.VMEM((blocks, WIDTH), f32),
            *[pltpu.VMEM(array.shape, array.dtype) for array in kept],
            pltpu.SemaphoreType.DMA((len(kept),)),
        ],
        compiler_params=pltpu.CompilerParams(vmem_limit_bytes=32 << 20),
        name="warp_and_pack",
    )(*[pltpu.with_memory_space_constraint(array, pltpu.HBM) for array in operands])


def place_kernel(parcel_ref, out_ref, slot_rows, spread_left, spread_right, corner_x_wide):
    f32, bf16 = jnp.float32, jnp.bfloat16
    slots = parcel_ref.shape[0]
    tracts, rows = out_ref.shape[0], PATCH // out_ref.shape[0]
    pitch = slots + 1

    for i in range(BLK):
        start = min(i * BLK, WIDTH - LANES)
        piece = parcel_ref[:, start : start + LANES].astype(f32)
        if start != i * BLK:
            piece = jnp.roll(piece, start - i * BLK, axis=1)
        slot_rows[pl.ds(i, slots, stride=BLK + 1), :] = piece
    tail = parcel_ref[:, WIDTH - LANES :].astype(f32)
    corner_x = tail[:, EXTRA + 1 : EXTRA + 2]
    corner_x_wide[...] = jnp.broadcast_to(corner_x, (slots, PATCH))
    by_slot = jnp.transpose(tail, (1, 0))
    corner_y = by_slot[EXTRA : EXTRA + 1, :]
    corner_x_row = by_slot[EXTRA + 1 : EXTRA + 2, :]
    weight = by_slot[EXTRA + 2 : EXTRA + 3, :]

    shift = (
        lax.broadcasted_iota(jnp.int32, (BLK, PATCH), 1)
        - lax.broadcasted_iota(jnp.int32, (BLK, PATCH), 0)
    ).astype(f32)
    batch = 16
    for first in range(0, slots, batch):
        placed = []
        for s in range(first, first + batch):
            column = jnp.where(shift == corner_x_wide[s : s + 1, :], 1.0, 0.0).astype(bf16)
            block = slot_rows[(BLK + 1) * s : (BLK + 1) * s + BLK, :][:, :BLK].astype(bf16)
            placed.append(jnp.dot(block, column, preferred_element_type=f32))
        for s in range(first, first + batch):
            spread_left[pl.ds(s, BLK, stride=pitch), :] = placed[s - first][:, :LANES]
            spread_right[pl.ds(s, BLK, stride=pitch), :] = placed[s - first][:, LANES:]

    above = lax.broadcasted_iota(jnp.int32, (PATCH, slots), 0).astype(f32) - corner_y
    flux = jnp.zeros((PATCH, PATCH), f32)
    depth = 2
    for i in range(0, BLK, depth):
        row = jnp.concatenate(
            [jnp.where(above == float(i + n), weight, 0.0).astype(bf16) for n in range(depth)], axis=1
        )
        across = jnp.concatenate(
            [
                jnp.concatenate(
                    [half[pitch * (i + n) : pitch * (i + n) + slots, :] for n in range(depth)], axis=0
                )
                for half in (spread_left, spread_right)
            ],
            axis=1,
        ).astype(bf16)
        flux += jnp.dot(row, across, preferred_element_type=f32)
    blank = jnp.zeros((6, PATCH), f32)
    for place, t in enumerate(tract_order(tracts)):
        corners = jnp.concatenate([corner_y - float(rows * t), corner_x_row], axis=1)
        weights = jnp.concatenate([weight, jnp.zeros_like(weight)], axis=1)
        parts = [flux[rows * t : rows * (t + 1), :], corners, weights, blank]
        out_ref[place] = jnp.concatenate(parts, axis=0).astype(bf16)


def place(parcel, tracts):
    slots = parcel.shape[0]
    f32 = jnp.float32
    return pl.pallas_call(
        place_kernel,
        out_shape=jax.ShapeDtypeStruct((tracts, PATCH // tracts + 8, PATCH), jnp.bfloat16),
        scratch_shapes=[
            pltpu.VMEM((slots * (BLK + 1), LANES), f32),
            pltpu.VMEM(((slots + 1) * BLK, LANES), f32),
            pltpu.VMEM(((slots + 1) * BLK, LANES), f32),
            pltpu.VMEM((slots, PATCH), f32),
        ],
        compiler_params=pltpu.CompilerParams(vmem_limit_bytes=24 << 20),
        name="place_in_patch",
    )(parcel)


def finish_kernel(parts_ref, flux_ref, cover_ref):
    f32, bf16 = jnp.float32, jnp.bfloat16
    rows, slots = flux_ref.shape[0], PATCH // 2
    y = lax.broadcasted_iota(jnp.int32, (rows, slots), 0).astype(f32)
    x = lax.broadcasted_iota(jnp.int32, (PATCH, slots), 0).astype(f32)
    flux = jnp.zeros((rows, PATCH), f32)
    cover = jnp.zeros((rows, PATCH), f32)
    for t in range(parts_ref.shape[0]):
        part = parts_ref[t].astype(f32)
        flux += part[:rows, :]
        extras = part[rows:, :]
        down = y - extras[0:1, :slots]
        across = x - extras[0:1, slots:]
        row = jnp.where((down >= 0.0) & (down < float(BLK)), extras[1:2, :slots], 0.0)
        column = jnp.where((across >= 0.0) & (across < float(BLK)), 1.0, 0.0)
        cover += lax.dot_general(
            row.astype(bf16),
            column.astype(bf16),
            (((1,), (1,)), ((), ())),
            preferred_element_type=f32,
        )
    flux_ref[...] = flux
    cover_ref[...] = cover


def finish(parts, tracts):
    out = jax.ShapeDtypeStruct((PATCH // tracts, PATCH), jnp.float32)
    return pl.pallas_call(
        finish_kernel,
        out_shape=(out, out),
        compiler_params=pltpu.CompilerParams(vmem_limit_bytes=16 << 20),
        name="finish",
    )(parts)


def per_device(images, coefficients, orders, resample, weights, routes, offsets):
    visit_count = lax.axis_size("visit")
    tract_count = lax.axis_size("tract")
    capacity = 2
    slot_count = visit_count * capacity
    parcel = warp_and_pack(
        images[0],
        coefficients[0],
        orders,
        resample[0],
        weights,
        routes[0],
        offsets[0],
        slot_count,
    )
    parcel = lax.all_to_all(
        parcel,
        "visit",
        split_axis=0,
        concat_axis=0,
        tiled=True,
        axis_index_groups=[visit_order(visit_count)],
    ).reshape(slot_count, WIDTH)
    parts = place(parcel, tract_count)
    parts = lax.all_to_all(
        parts,
        "tract",
        split_axis=0,
        concat_axis=0,
        tiled=True,
        axis_index_groups=[tract_order(tract_count)],
    )
    flux, cover = finish(parts, tract_count)
    return (flux[None], cover[None])


def solution(mesh):
    in_specs = (
        P("tract", "visit", None),
        P("tract", "visit", None),
        P("tract", "visit"),
        P("tract", "visit", None),
        P("tract", "visit"),
        P("tract", "visit", None),
        P("tract", "visit", None, None),
    )
    out_specs = (P("visit", "tract", None), P("visit", "tract", None))
    return jax.shard_map(
        per_device, mesh=mesh, in_specs=in_specs, out_specs=out_specs, check_vma=False
    )
```

```python
import functools

import jax
import jax.numpy as jnp
import numpy as np
from jax import lax
from jax.experimental import pallas as pl
from jax.experimental.pallas import tpu as pltpu
from jax.sharding import PartitionSpec as P

KSIZE = 41
NBASIS = 16
NTERMS = 6
TOP = 2
BLK = 40
PATCH = 256
HALF = 20
BLKIN = 80
LANES = 128
WIDTH = 1664
EXTRA = 1600 % LANES

SIGMAS = (0.7, 1.5, 3.0, 2.0)
POWERS = (0, 0, 0, 1)
COLUMN_AT = (0, 40, 80, 128)


DEEP = 16
START = (2, 9)
FIRST = 5


def visit_order(count):
    wide = count // DEEP
    return [
        (x + START[0]) % wide * DEEP + (z + START[1]) % DEEP for x in range(wide) for z in range(DEEP)
    ]


def tract_order(count):
    return [(t + FIRST) % count for t in range(count)]


def constant_tables():
    difference = np.arange(BLKIN)[None, :] - np.arange(BLK)[:, None]
    inside = (difference >= 0) & (difference < KSIZE)
    shifted = (difference - HALF).astype(np.float32)
    taps = np.arange(KSIZE, dtype=np.float32) - np.float32(HALF)
    tables = []
    for sigma, power in zip(SIGMAS, POWERS):

        def profile(offset):
            value = np.exp(-offset * offset / np.float32(2.0 * sigma * sigma)).astype(np.float32)
            if power == 1:
                value = value * offset / np.float32(sigma)
            return value.astype(np.float32)

        total = np.sum(np.abs(profile(taps)), dtype=np.float32)
        tables.append(np.where(inside, profile(shifted) / total, np.float32(0.0)))
    held = np.zeros((4 * BLK + LANES, 2 * LANES), np.float32)
    held[: 4 * BLK, :BLKIN] = np.concatenate(tables, axis=0)
    for c, at in enumerate(COLUMN_AT):
        held[4 * BLK : 4 * BLK + BLKIN, at : at + BLK] = tables[c].T
    return jnp.asarray(held, jnp.bfloat16)


def warp_kernel(
    images_ref,
    coefficients_ref,
    orders_ref,
    resample_ref,
    weights_ref,
    routes_ref,
    offsets_ref,
    tables_ref,
    out_ref,
    image_rows,
    resample_rows,
    planes,
    warped_rows,
    flat,
    *held,
):
    f32, bf16 = jnp.float32, jnp.bfloat16
    *held, arrival = held
    sources = (
        images_ref,
        resample_ref,
        coefficients_ref,
        orders_ref,
        weights_ref,
        routes_ref,
        offsets_ref,
        tables_ref,
    )
    copies = [
        pltpu.make_async_copy(source, kept, arrival.at[number])
        for number, (source, kept) in enumerate(zip(sources, held, strict=True))
    ]
    for copy in copies:
        copy.start()
    (
        images_ref,
        resample_ref,
        coefficients_ref,
        orders_ref,
        weights_ref,
        routes_ref,
        offsets_ref,
        tables_ref,
    ) = held
    copies[0].wait()
    blocks = images_ref.shape[0]
    wide = 2 * LANES

    for x in range(BLKIN):
        start = min(x * BLKIN, BLKIN * BLKIN - LANES)
        piece = images_ref[:, start : start + LANES].astype(f32)
        if start != x * BLKIN:
            piece = jnp.roll(piece, start - x * BLKIN, axis=1)
        image_rows[pl.ds(x, blocks, stride=BLKIN + 1), :] = piece
    copies[1].wait()
    for copy in copies[2:]:
        copy.wait()
    for x in range(2 * BLK):
        start = min(x * BLK, 2 * BLK * BLK - LANES)
        piece = resample_ref[:, start : start + LANES].astype(f32)
        if start != x * BLK:
            piece = jnp.roll(piece, start - x * BLK, axis=1)
        resample_rows[pl.ds(x, blocks, stride=2 * BLK + 1), :] = piece

    terms = jnp.concatenate(
        [coefficients_ref[:, 4 * NTERMS * r : 4 * NTERMS * (r + 1)] for r in range(4)], axis=0
    )
    term_id = lax.broadcasted_iota(jnp.int32, (4 * NTERMS, wide), 0)
    lane = lax.broadcasted_iota(jnp.int32, (4 * NTERMS, wide), 1)
    column_kernel = sum((lane >= at).astype(jnp.int32) for at in COLUMN_AT[1:])
    spread = jnp.concatenate(
        [
            jnp.where(term_id == NTERMS * column_kernel + m, 1.0, 0.0).astype(bf16)
            for m in range(NTERMS)
        ],
        axis=1,
    )
    spread = jnp.dot(terms, spread, preferred_element_type=f32)
    lane = lax.broadcasted_iota(jnp.int32, (blocks, blocks), 1)
    sublane = lax.broadcasted_iota(jnp.int32, (blocks, blocks), 0)
    order = jnp.sum(
        jnp.where(lane == sublane, orders_ref[...].astype(f32), 0.0), axis=1, keepdims=True
    )
    order = jnp.concatenate([order] * 4, axis=0)
    first, second = order >= 1.0, order >= 2.0
    term = [spread[:, wide * m : wide * (m + 1)] for m in range(NTERMS)]
    term = (
        term[:1]
        + [jnp.where(first, t, 0.0) for t in term[1:3]]
        + [jnp.where(second, t, 0.0) for t in term[3:]]
    )
    lane = lax.broadcasted_iota(jnp.int32, (1, wide), 1)
    within = lane
    for at in COLUMN_AT[1:]:
        within = jnp.where(lane >= at, lane - at, within)
    across = (2.0 * within.astype(f32) + 1.0) / BLK - 1.0
    planes[:, :wide] = term[0] + across * (term[2] + across * term[5])
    planes[:, wide : 2 * wide] = term[1] + across * term[4]
    planes[:, 2 * wide :] = term[3]

    row_id = lax.broadcasted_iota(jnp.int32, (BLK, wide), 0).astype(f32)
    down = (2.0 * row_id + 1.0) / BLK - 1.0

    stacked = jnp.concatenate(
        [
            image_rows[(BLKIN + 1) * g : (BLKIN + 1) * g + BLKIN, :]
            for g in range(blocks)
        ],
        axis=1,
    ).astype(bf16)
    smooth = jnp.dot(tables_ref[: 4 * BLK, :BLKIN], stacked, preferred_element_type=f32).astype(bf16)
    responses = [
        jnp.dot(
            smooth[:, LANES * g : LANES * (g + 1)],
            tables_ref[4 * BLK :, :],
            preferred_element_type=f32,
        )
        for g in range(blocks)
    ]
    matched = []
    for g in range(blocks):
        total = jnp.zeros((BLK, wide), f32)
        for r in range(4):
            plane = planes[r * blocks + g : r * blocks + g + 1, :]
            weight = plane[:, :wide] + down * (
                plane[:, wide : 2 * wide] + down * plane[:, 2 * wide :]
            )
            total = total + weight * responses[g][BLK * r : BLK * (r + 1), :]
        low, high = total[:, :LANES], total[:, LANES:]
        folded = (
            low
            + high
            + pltpu.roll(low, LANES - BLK, axis=1)
            + pltpu.roll(low, LANES - 2 * BLK, axis=1)
        )
        matched.append(folded[:, :BLK].astype(bf16))
    halfway = [
        jnp.dot(
            resample_rows[(2 * BLK + 1) * g : (2 * BLK + 1) * g + BLK, :][:, :BLK].astype(bf16),
            matched[g],
            preferred_element_type=f32,
        ).astype(bf16)
        for g in range(blocks)
    ]
    warped = [
        lax.dot_general(
            halfway[g],
            resample_rows[(2 * BLK + 1) * g + BLK : (2 * BLK + 1) * (g + 1) - 1, :][:, :BLK].astype(bf16),
            (((1,), (1,)), ((), ())),
            preferred_element_type=f32,
        )
        for g in range(blocks)
    ]
    for g in range(blocks):
        warped_rows[(BLK + 1) * g : (BLK + 1) * g + BLK, 0:BLK] = warped[g]
    flat[:, 12 * LANES :] = jnp.zeros((blocks, LANES), f32)
    for i in range(BLK):
        flat[:, BLK * i : BLK * (i + 1)] = warped_rows[pl.ds(i, blocks, stride=BLK + 1), 0:BLK]
    pixels = flat[...].astype(bf16)

    slots, pairs = out_ref.shape[0] * out_ref.shape[1], TOP * blocks
    patch = jnp.concatenate([routes_ref[k : k + 1, :] for k in range(TOP)], axis=1)
    slot = lax.broadcasted_iota(jnp.int32, (slots, pairs), 0)
    place = slot // 2
    member = ((place + DEEP * START[0]) & (-DEEP & (slots // 2 - 1))) | (
        (place + START[1]) & (DEEP - 1)
    )
    hit = jnp.where(patch == member, 1.0, 0.0)
    before = lax.broadcasted_iota(jnp.int32, (pairs, pairs), 0)
    after = lax.broadcasted_iota(jnp.int32, (pairs, pairs), 1)
    rank = jnp.dot(
        hit.astype(bf16),
        jnp.where(before < after, 1.0, 0.0).astype(bf16),
        preferred_element_type=f32,
    )
    pick = jnp.where(rank == (slot % 2).astype(f32), hit, 0.0).astype(bf16)
    packed = jnp.dot(
        pick, jnp.concatenate([pixels] * TOP, axis=0), preferred_element_type=f32
    )
    column = lax.broadcasted_iota(jnp.int32, (LANES, pairs), 0) - EXTRA
    corner_y = jnp.concatenate([offsets_ref[k, 0:1, :] for k in range(TOP)], axis=1).astype(f32)
    corner_x = jnp.concatenate([offsets_ref[k, 1:2, :] for k in range(TOP)], axis=1).astype(f32)
    weight = jnp.concatenate([weights_ref[...].astype(f32)] * TOP, axis=1)
    extras = jnp.where(
        column == 0,
        corner_y,
        jnp.where(column == 1, corner_x, jnp.where(column == 2, weight, 0.0)),
    ).astype(bf16)
    tail = lax.dot_general(pick, extras, (((1,), (1,)), ((), ())), preferred_element_type=f32)
    packed = jnp.concatenate([packed[:, : 12 * LANES], packed[:, 12 * LANES :] + tail], axis=1)
    out_ref[...] = packed.astype(bf16).reshape(out_ref.shape)


def warp_and_pack(images, coefficients, orders, resample, weights, routes, offsets, slots):
    blocks = images.shape[0]
    f32 = jnp.float32
    operands = (
        images,
        coefficients,
        orders,
        resample,
        weights,
        jnp.transpose(routes, (1, 0)),
        jnp.transpose(offsets, (1, 2, 0)),
        constant_tables(),
    )
    kept = [operands[n] for n in (0, 3, 1, 2, 4, 5, 6, 7)]
    return pl.pallas_call(
        warp_kernel,
        out_shape=jax.ShapeDtypeStruct((slots // 2, 2, WIDTH), jnp.bfloat16),
        in_specs=[pl.BlockSpec(memory_space=pl.ANY)] * len(operands),
        scratch_shapes=[
            pltpu.VMEM(((blocks + 1) * (BLKIN + 1), LANES), f32),
            pltpu.VMEM(((blocks + 1) * (2 * BLK + 1), LANES), f32),
            pltpu.VMEM((blocks * 4, 3 * 2 * LANES), f32),
            pltpu.VMEM(((blocks + 1) * (BLK + 1), LANES), f32),
            pltpu.VMEM((blocks, WIDTH), f32),
            *[pltpu.VMEM(array.shape, array.dtype) for array in kept],
            pltpu.SemaphoreType.DMA((len(kept),)),
        ],
        compiler_params=pltpu.CompilerParams(vmem_limit_bytes=32 << 20),
        name="warp_and_pack",
    )(*[pltpu.with_memory_space_constraint(array, pltpu.HBM) for array in operands])


def place_kernel(parcel_ref, out_ref, slot_rows, spread_left, spread_right, corner_x_wide):
    f32, bf16 = jnp.float32, jnp.bfloat16
    slots = parcel_ref.shape[0]
    tracts, rows = out_ref.shape[0], PATCH // out_ref.shape[0]
    pitch = slots + 1

    for i in range(BLK):
        start = min(i * BLK, WIDTH - LANES)
        piece = parcel_ref[:, start : start + LANES].astype(f32)
        if start != i * BLK:
            piece = jnp.roll(piece, start - i * BLK, axis=1)
        slot_rows[pl.ds(i, slots, stride=BLK + 1), :] = piece
    tail = parcel_ref[:, WIDTH - LANES :].astype(f32)
    corner_x = tail[:, EXTRA + 1 : EXTRA + 2]
    corner_x_wide[...] = jnp.broadcast_to(corner_x, (slots, PATCH))
    by_slot = jnp.transpose(tail, (1, 0))
    corner_y = by_slot[EXTRA : EXTRA + 1, :]
    corner_x_row = by_slot[EXTRA + 1 : EXTRA + 2, :]
    weight = by_slot[EXTRA + 2 : EXTRA + 3, :]

    shift = (
        lax.broadcasted_iota(jnp.int32, (BLK, PATCH), 1)
        - lax.broadcasted_iota(jnp.int32, (BLK, PATCH), 0)
    ).astype(f32)
    batch = 16
    for first in range(0, slots, batch):
        placed = []
        for s in range(first, first + batch):
            column = jnp.where(shift == corner_x_wide[s : s + 1, :], 1.0, 0.0).astype(bf16)
            block = slot_rows[(BLK + 1) * s : (BLK + 1) * s + BLK, :][:, :BLK].astype(bf16)
            placed.append(jnp.dot(block, column, preferred_element_type=f32))
        for s in range(first, first + batch):
            spread_left[pl.ds(s, BLK, stride=pitch), :] = placed[s - first][:, :LANES]
            spread_right[pl.ds(s, BLK, stride=pitch), :] = placed[s - first][:, LANES:]

    above = lax.broadcasted_iota(jnp.int32, (PATCH, slots), 0).astype(f32) - corner_y
    flux = jnp.zeros((PATCH, PATCH), f32)
    depth = 2
    for i in range(0, BLK, depth):
        row = jnp.concatenate(
            [jnp.where(above == float(i + n), weight, 0.0).astype(bf16) for n in range(depth)], axis=1
        )
        across = jnp.concatenate(
            [
                jnp.concatenate(
                    [half[pitch * (i + n) : pitch * (i + n) + slots, :] for n in range(depth)], axis=0
                )
                for half in (spread_left, spread_right)
            ],
            axis=1,
        ).astype(bf16)
        flux += jnp.dot(row, across, preferred_element_type=f32)
    blank = jnp.zeros((6, PATCH), f32)
    for place, t in enumerate(tract_order(tracts)):
        corners = jnp.concatenate([corner_y - float(rows * t), corner_x_row], axis=1)
        weights = jnp.concatenate([weight, jnp.zeros_like(weight)], axis=1)
        parts = [flux[rows * t : rows * (t + 1), :], corners, weights, blank]
        out_ref[place] = jnp.concatenate(parts, axis=0).astype(bf16)


def place(parcel, tracts):
    slots = parcel.shape[0]
    f32 = jnp.float32
    return pl.pallas_call(
        place_kernel,
        out_shape=jax.ShapeDtypeStruct((tracts, PATCH // tracts + 8, PATCH), jnp.bfloat16),
        scratch_shapes=[
            pltpu.VMEM(((slots + 1) * (BLK + 1), LANES), f32),
            pltpu.VMEM(((slots + 1) * (BLK + 1), LANES), f32),
            pltpu.VMEM(((slots + 1) * (BLK + 1), LANES), f32),
            pltpu.VMEM((slots, PATCH), f32),
        ],
        compiler_params=pltpu.CompilerParams(vmem_limit_bytes=24 << 20),
        name="place_in_patch",
    )(parcel)


def finish_kernel(parts_ref, flux_ref, cover_ref):
    f32, bf16 = jnp.float32, jnp.bfloat16
    rows, slots = flux_ref.shape[0], PATCH // 2
    y = lax.broadcasted_iota(jnp.int32, (rows, slots), 0).astype(f32)
    x = lax.broadcasted_iota(jnp.int32, (PATCH, slots), 0).astype(f32)
    flux = jnp.zeros((rows, PATCH), f32)
    cover = jnp.zeros((rows, PATCH), f32)
    for t in range(parts_ref.shape[0]):
        part = parts_ref[t].astype(f32)
        flux += part[:rows, :]
        extras = part[rows:, :]
        down = y - extras[0:1, :slots]
        across = x - extras[0:1, slots:]
        row = jnp.where((down >= 0.0) & (down < float(BLK)), extras[1:2, :slots], 0.0)
        column = jnp.where((across >= 0.0) & (across < float(BLK)), 1.0, 0.0)
        cover += lax.dot_general(
            row.astype(bf16),
            column.astype(bf16),
            (((1,), (1,)), ((), ())),
            preferred_element_type=f32,
        )
    flux_ref[...] = flux
    cover_ref[...] = cover


def finish(parts, tracts):
    out = jax.ShapeDtypeStruct((PATCH // tracts, PATCH), jnp.float32)
    return pl.pallas_call(
        finish_kernel,
        out_shape=(out, out),
        compiler_params=pltpu.CompilerParams(vmem_limit_bytes=16 << 20),
        name="finish",
    )(parts)


def per_device(images, coefficients, orders, resample, weights, routes, offsets):
    visit_count = lax.axis_size("visit")
    tract_count = lax.axis_size("tract")
    capacity = 2
    slot_count = visit_count * capacity
    parcel = warp_and_pack(
        images[0],
        coefficients[0],
        orders,
        resample[0],
        weights,
        routes[0],
        offsets[0],
        slot_count,
    )
    parcel = lax.all_to_all(
        parcel,
        "visit",
        split_axis=0,
        concat_axis=0,
        tiled=True,
        axis_index_groups=[visit_order(visit_count)],
    ).reshape(slot_count, WIDTH)
    parts = place(parcel, tract_count)
    parts = lax.all_to_all(
        parts,
        "tract",
        split_axis=0,
        concat_axis=0,
        tiled=True,
        axis_index_groups=[tract_order(tract_count)],
    )
    flux, cover = finish(parts, tract_count)
    return (flux[None], cover[None])


def solution(mesh):
    in_specs = (
        P("tract", "visit", None),
        P("tract", "visit", None),
        P("tract", "visit"),
        P("tract", "visit", None),
        P("tract", "visit"),
        P("tract", "visit", None),
        P("tract", "visit", None, None),
    )
    out_specs = (P("visit", "tract", None), P("visit", "tract", None))
    return jax.shard_map(
        per_device, mesh=mesh, in_specs=in_specs, out_specs=out_specs, check_vma=False
    )
```

```python
import functools

import jax
import jax.numpy as jnp
import numpy as np
from jax import lax
from jax.experimental import pallas as pl
from jax.experimental.pallas import tpu as pltpu
from jax.sharding import PartitionSpec as P

KSIZE = 41
NBASIS = 16
NTERMS = 6
TOP = 2
BLK = 40
PATCH = 256
HALF = 20
BLKIN = 80
LANES = 128
WIDTH = 1664
EXTRA = 1600 % LANES

SIGMAS = (0.7, 1.5, 3.0, 2.0)
POWERS = (0, 0, 0, 1)
COLUMN_AT = (0, 40, 80, 128)


DEEP = 16
START = (2, 9)
FIRST = 5


def visit_order(count):
    wide = count // DEEP
    return [
        (x + START[0]) % wide * DEEP + (z + START[1]) % DEEP for x in range(wide) for z in range(DEEP)
    ]


def tract_order(count):
    return [(t + FIRST) % count for t in range(count)]


def constant_tables():
    difference = np.arange(BLKIN)[None, :] - np.arange(BLK)[:, None]
    inside = (difference >= 0) & (difference < KSIZE)
    shifted = (difference - HALF).astype(np.float32)
    taps = np.arange(KSIZE, dtype=np.float32) - np.float32(HALF)
    tables = []
    for sigma, power in zip(SIGMAS, POWERS):

        def profile(offset):
            value = np.exp(-offset * offset / np.float32(2.0 * sigma * sigma)).astype(np.float32)
            if power == 1:
                value = value * offset / np.float32(sigma)
            return value.astype(np.float32)

        total = np.sum(np.abs(profile(taps)), dtype=np.float32)
        tables.append(np.where(inside, profile(shifted) / total, np.float32(0.0)))
    held = np.zeros((4 * BLK + LANES, 2 * LANES), np.float32)
    held[: 4 * BLK, :BLKIN] = np.concatenate(tables, axis=0)
    for c, at in enumerate(COLUMN_AT):
        held[4 * BLK : 4 * BLK + BLKIN, at : at + BLK] = tables[c].T
    return jnp.asarray(held, jnp.bfloat16)


def warp_kernel(
    images_ref,
    coefficients_ref,
    orders_ref,
    resample_ref,
    weights_ref,
    routes_ref,
    offsets_ref,
    tables_ref,
    out_ref,
    image_rows,
    resample_rows,
    planes,
    warped_rows,
    flat,
    *held,
):
    f32, bf16 = jnp.float32, jnp.bfloat16
    *held, arrival = held
    sources = (
        images_ref,
        resample_ref,
        coefficients_ref,
        orders_ref,
        weights_ref,
        routes_ref,
        offsets_ref,
        tables_ref,
    )
    copies = [
        pltpu.make_async_copy(source, kept, arrival.at[number])
        for number, (source, kept) in enumerate(zip(sources, held, strict=True))
    ]
    for copy in copies:
        copy.start()
    (
        images_ref,
        resample_ref,
        coefficients_ref,
        orders_ref,
        weights_ref,
        routes_ref,
        offsets_ref,
        tables_ref,
    ) = held
    copies[0].wait()
    blocks = images_ref.shape[0]
    wide = 2 * LANES

    for x in range(BLKIN):
        start = min(x * BLKIN, BLKIN * BLKIN - LANES)
        piece = images_ref[:, start : start + LANES].astype(f32)
        if start != x * BLKIN:
            piece = jnp.roll(piece, start - x * BLKIN, axis=1)
        image_rows[pl.ds(x, blocks, stride=BLKIN + 1), :] = piece
    copies[1].wait()
    for copy in copies[2:]:
        copy.wait()
    for x in range(2 * BLK):
        start = min(x * BLK, 2 * BLK * BLK - LANES)
        piece = resample_ref[:, start : start + LANES].astype(f32)
        if start != x * BLK:
            piece = jnp.roll(piece, start - x * BLK, axis=1)
        resample_rows[pl.ds(x, blocks, stride=2 * BLK + 1), :] = piece

    terms = jnp.concatenate(
        [coefficients_ref[:, 4 * NTERMS * r : 4 * NTERMS * (r + 1)] for r in range(4)], axis=0
    )
    term_id = lax.broadcasted_iota(jnp.int32, (4 * NTERMS, wide), 0)
    lane = lax.broadcasted_iota(jnp.int32, (4 * NTERMS, wide), 1)
    column_kernel = sum((lane >= at).astype(jnp.int32) for at in COLUMN_AT[1:])
    spread = jnp.concatenate(
        [
            jnp.where(term_id == NTERMS * column_kernel + m, 1.0, 0.0).astype(bf16)
            for m in range(NTERMS)
        ],
        axis=1,
    )
    spread = jnp.dot(terms, spread, preferred_element_type=f32)
    lane = lax.broadcasted_iota(jnp.int32, (blocks, blocks), 1)
    sublane = lax.broadcasted_iota(jnp.int32, (blocks, blocks), 0)
    order = jnp.sum(
        jnp.where(lane == sublane, orders_ref[...].astype(f32), 0.0), axis=1, keepdims=True
    )
    order = jnp.concatenate([order] * 4, axis=0)
    first, second = order >= 1.0, order >= 2.0
    term = [spread[:, wide * m : wide * (m + 1)] for m in range(NTERMS)]
    term = (
        term[:1]
        + [jnp.where(first, t, 0.0) for t in term[1:3]]
        + [jnp.where(second, t, 0.0) for t in term[3:]]
    )
    lane = lax.broadcasted_iota(jnp.int32, (1, wide), 1)
    within = lane
    for at in COLUMN_AT[1:]:
        within = jnp.where(lane >= at, lane - at, within)
    across = (2.0 * within.astype(f32) + 1.0) / BLK - 1.0
    planes[:, :wide] = term[0] + across * (term[2] + across * term[5])
    planes[:, wide : 2 * wide] = term[1] + across * term[4]
    planes[:, 2 * wide :] = term[3]

    row_id = lax.broadcasted_iota(jnp.int32, (BLK, wide), 0).astype(f32)
    down = (2.0 * row_id + 1.0) / BLK - 1.0

    stacked = jnp.concatenate(
        [
            image_rows[(BLKIN + 1) * g : (BLKIN + 1) * g + BLKIN, :]
            for g in range(blocks)
        ],
        axis=1,
    ).astype(bf16)
    smooth = jnp.dot(tables_ref[: 4 * BLK, :BLKIN], stacked, preferred_element_type=f32).astype(bf16)
    responses = [
        jnp.dot(
            smooth[:, LANES * g : LANES * (g + 1)],
            tables_ref[4 * BLK :, :],
            preferred_element_type=f32,
        )
        for g in range(blocks)
    ]
    matched = []
    for g in range(blocks):
        total = jnp.zeros((BLK, wide), f32)
        for r in range(4):
            plane = planes[r * blocks + g : r * blocks + g + 1, :]
            weight = plane[:, :wide] + down * (
                plane[:, wide : 2 * wide] + down * plane[:, 2 * wide :]
            )
            total = total + weight * responses[g][BLK * r : BLK * (r + 1), :]
        low, high = total[:, :LANES], total[:, LANES:]
        folded = (
            low
            + high
            + pltpu.roll(low, LANES - BLK, axis=1)
            + pltpu.roll(low, LANES - 2 * BLK, axis=1)
        )
        matched.append(folded[:, :BLK].astype(bf16))
    halfway = [
        jnp.dot(
            resample_rows[(2 * BLK + 1) * g : (2 * BLK + 1) * g + BLK, :][:, :BLK].astype(bf16),
            matched[g],
            preferred_element_type=f32,
        ).astype(bf16)
        for g in range(blocks)
    ]
    warped = [
        lax.dot_general(
            halfway[g],
            resample_rows[(2 * BLK + 1) * g + BLK : (2 * BLK + 1) * (g + 1) - 1, :][:, :BLK].astype(bf16),
            (((1,), (1,)), ((), ())),
            preferred_element_type=f32,
        )
        for g in range(blocks)
    ]
    for g in range(blocks):
        warped_rows[(BLK + 1) * g : (BLK + 1) * g + BLK, 0:BLK] = warped[g]
    flat[:, 12 * LANES :] = jnp.zeros((blocks, LANES), f32)
    for i in range(BLK):
        flat[:, BLK * i : BLK * (i + 1)] = warped_rows[pl.ds(i, blocks, stride=BLK + 1), 0:BLK]
    pixels = flat[...].astype(bf16)

    slots, pairs = out_ref.shape[0], TOP * blocks
    patch = jnp.concatenate([routes_ref[k : k + 1, :] for k in range(TOP)], axis=1)
    slot = lax.broadcasted_iota(jnp.int32, (slots, pairs), 0)
    place = slot // 2
    member = ((place + DEEP * START[0]) & (-DEEP & (slots // 2 - 1))) | (
        (place + START[1]) & (DEEP - 1)
    )
    hit = jnp.where(patch == member, 1.0, 0.0)
    before = lax.broadcasted_iota(jnp.int32, (pairs, pairs), 0)
    after = lax.broadcasted_iota(jnp.int32, (pairs, pairs), 1)
    rank = jnp.dot(
        hit.astype(bf16),
        jnp.where(before < after, 1.0, 0.0).astype(bf16),
        preferred_element_type=f32,
    )
    pick = jnp.where(rank == (slot % 2).astype(f32), hit, 0.0).astype(bf16)
    packed = jnp.dot(
        pick, jnp.concatenate([pixels] * TOP, axis=0), preferred_element_type=f32
    )
    column = lax.broadcasted_iota(jnp.int32, (LANES, pairs), 0) - EXTRA
    corner_y = jnp.concatenate([offsets_ref[k, 0:1, :] for k in range(TOP)], axis=1).astype(f32)
    corner_x = jnp.concatenate([offsets_ref[k, 1:2, :] for k in range(TOP)], axis=1).astype(f32)
    weight = jnp.concatenate([weights_ref[...].astype(f32)] * TOP, axis=1)
    extras = jnp.where(
        column == 0,
        corner_y,
        jnp.where(column == 1, corner_x, jnp.where(column == 2, weight, 0.0)),
    ).astype(bf16)
    tail = lax.dot_general(pick, extras, (((1,), (1,)), ((), ())), preferred_element_type=f32)
    packed = jnp.concatenate([packed[:, : 12 * LANES], packed[:, 12 * LANES :] + tail], axis=1)
    out_ref[...] = packed.astype(bf16)


def warp_and_pack(images, coefficients, orders, resample, weights, routes, offsets, slots):
    blocks = images.shape[0]
    f32 = jnp.float32
    operands = (
        images,
        coefficients,
        orders,
        resample,
        weights,
        jnp.transpose(routes, (1, 0)),
        jnp.transpose(offsets, (1, 2, 0)),
        constant_tables(),
    )
    kept = [operands[n] for n in (0, 3, 1, 2, 4, 5, 6, 7)]
    return pl.pallas_call(
        warp_kernel,
        out_shape=jax.ShapeDtypeStruct((slots, WIDTH), jnp.bfloat16),
        in_specs=[pl.BlockSpec(memory_space=pl.ANY)] * len(operands),
        scratch_shapes=[
            pltpu.VMEM(((blocks + 1) * (BLKIN + 1), LANES), f32),
            pltpu.VMEM(((blocks + 1) * (2 * BLK + 1), LANES), f32),
            pltpu.VMEM((blocks * 4, 3 * 2 * LANES), f32),
            pltpu.VMEM(((blocks + 1) * (BLK + 1), LANES), f32),
            pltpu.VMEM((blocks, WIDTH), f32),
            *[pltpu.VMEM(array.shape, array.dtype) for array in kept],
            pltpu.SemaphoreType.DMA((len(kept),)),
        ],
        compiler_params=pltpu.CompilerParams(vmem_limit_bytes=32 << 20),
        name="warp_and_pack",
    )(*[pltpu.with_memory_space_constraint(array, pltpu.HBM) for array in operands])


def place_kernel(parcel_ref, out_ref, slot_rows, spread_left, spread_right, corner_x_wide):
    f32, bf16 = jnp.float32, jnp.bfloat16
    slots = parcel_ref.shape[0]
    tracts, rows = out_ref.shape[0], PATCH // out_ref.shape[0]
    pitch = slots + 1

    for i in range(BLK):
        start = min(i * BLK, WIDTH - LANES)
        piece = parcel_ref[:, start : start + LANES].astype(f32)
        if start != i * BLK:
            piece = jnp.roll(piece, start - i * BLK, axis=1)
        slot_rows[pl.ds(i, slots, stride=BLK + 1), :] = piece
    tail = parcel_ref[:, WIDTH - LANES :].astype(f32)
    corner_x = tail[:, EXTRA + 1 : EXTRA + 2]
    corner_x_wide[...] = jnp.broadcast_to(corner_x, (slots, PATCH))
    by_slot = jnp.transpose(tail, (1, 0))
    corner_y = by_slot[EXTRA : EXTRA + 1, :]
    corner_x_row = by_slot[EXTRA + 1 : EXTRA + 2, :]
    weight = by_slot[EXTRA + 2 : EXTRA + 3, :]

    shift = (
        lax.broadcasted_iota(jnp.int32, (BLK, PATCH), 1)
        - lax.broadcasted_iota(jnp.int32, (BLK, PATCH), 0)
    ).astype(f32)
    batch = 32
    for first in range(0, slots, batch):
        placed = []
        for s in range(first, first + batch):
            column = jnp.where(shift == corner_x_wide[s : s + 1, :], 1.0, 0.0).astype(bf16)
            block = slot_rows[(BLK + 1) * s : (BLK + 1) * s + BLK, :][:, :BLK].astype(bf16)
            placed.append(jnp.dot(block, column, preferred_element_type=f32))
        for s in range(first, first + batch):
            spread_left[pl.ds(s, BLK, stride=pitch), :] = placed[s - first][:, :LANES]
            spread_right[pl.ds(s, BLK, stride=pitch), :] = placed[s - first][:, LANES:]

    above = lax.broadcasted_iota(jnp.int32, (PATCH, slots), 0).astype(f32) - corner_y
    flux = jnp.zeros((PATCH, PATCH), f32)
    depth = 2
    for i in range(0, BLK, depth):
        row = jnp.concatenate(
            [jnp.where(above == float(i + n), weight, 0.0).astype(bf16) for n in range(depth)], axis=1
        )
        across = jnp.concatenate(
            [
                jnp.concatenate(
                    [half[pitch * (i + n) : pitch * (i + n) + slots, :] for n in range(depth)], axis=0
                )
                for half in (spread_left, spread_right)
            ],
            axis=1,
        ).astype(bf16)
        flux += jnp.dot(row, across, preferred_element_type=f32)
    blank = jnp.zeros((6, PATCH), f32)
    for place, t in enumerate(tract_order(tracts)):
        corners = jnp.concatenate([corner_y - float(rows * t), corner_x_row], axis=1)
        weights = jnp.concatenate([weight, jnp.zeros_like(weight)], axis=1)
        parts = [flux[rows * t : rows * (t + 1), :], corners, weights, blank]
        out_ref[place] = jnp.concatenate(parts, axis=0).astype(bf16)


def place(parcel, tracts):
    slots = parcel.shape[0]
    f32 = jnp.float32
    return pl.pallas_call(
        place_kernel,
        out_shape=jax.ShapeDtypeStruct((tracts, PATCH // tracts + 8, PATCH), jnp.bfloat16),
        scratch_shapes=[
            pltpu.VMEM(((slots + 1) * (BLK + 1), LANES), f32),
            pltpu.VMEM(((slots + 1) * (BLK + 1), LANES), f32),
            pltpu.VMEM(((slots + 1) * (BLK + 1), LANES), f32),
            pltpu.VMEM((slots, PATCH), f32),
        ],
        compiler_params=pltpu.CompilerParams(vmem_limit_bytes=24 << 20),
        name="place_in_patch",
    )(parcel)


def finish_kernel(parts_ref, flux_ref, cover_ref):
    f32, bf16 = jnp.float32, jnp.bfloat16
    rows, slots = flux_ref.shape[0], PATCH // 2
    y = lax.broadcasted_iota(jnp.int32, (rows, slots), 0).astype(f32)
    x = lax.broadcasted_iota(jnp.int32, (PATCH, slots), 0).astype(f32)
    flux = jnp.zeros((rows, PATCH), f32)
    cover = jnp.zeros((rows, PATCH), f32)
    for t in range(parts_ref.shape[0]):
        part = parts_ref[t].astype(f32)
        flux += part[:rows, :]
        extras = part[rows:, :]
        down = y - extras[0:1, :slots]
        across = x - extras[0:1, slots:]
        row = jnp.where((down >= 0.0) & (down < float(BLK)), extras[1:2, :slots], 0.0)
        column = jnp.where((across >= 0.0) & (across < float(BLK)), 1.0, 0.0)
        cover += lax.dot_general(
            row.astype(bf16),
            column.astype(bf16),
            (((1,), (1,)), ((), ())),
            preferred_element_type=f32,
        )
    flux_ref[...] = flux
    cover_ref[...] = cover


def finish(parts, tracts):
    out = jax.ShapeDtypeStruct((PATCH // tracts, PATCH), jnp.float32)
    return pl.pallas_call(
        finish_kernel,
        out_shape=(out, out),
        compiler_params=pltpu.CompilerParams(vmem_limit_bytes=16 << 20),
        name="finish",
    )(parts)


def per_device(images, coefficients, orders, resample, weights, routes, offsets):
    visit_count = lax.axis_size("visit")
    tract_count = lax.axis_size("tract")
    capacity = 2
    slot_count = visit_count * capacity
    parcel = warp_and_pack(
        images[0],
        coefficients[0],
        orders,
        resample[0],
        weights,
        routes[0],
        offsets[0],
        slot_count,
    )
    parcel = lax.all_to_all(
        parcel,
        "visit",
        split_axis=0,
        concat_axis=0,
        tiled=True,
        axis_index_groups=[visit_order(visit_count)],
    )
    parts = place(parcel, tract_count)
    parts = lax.all_to_all(
        parts,
        "tract",
        split_axis=0,
        concat_axis=0,
        tiled=True,
        axis_index_groups=[tract_order(tract_count)],
    )
    flux, cover = finish(parts, tract_count)
    return (flux[None], cover[None])


def solution(mesh):
    in_specs = (
        P("tract", "visit", None),
        P("tract", "visit", None),
        P("tract", "visit"),
        P("tract", "visit", None),
        P("tract", "visit"),
        P("tract", "visit", None),
        P("tract", "visit", None, None),
    )
    out_specs = (P("visit", "tract", None), P("visit", "tract", None))
    return jax.shard_map(
        per_device, mesh=mesh, in_specs=in_specs, out_specs=out_specs, check_vma=False
    )
```

```python
import functools

import jax
import jax.numpy as jnp
import numpy as np
from jax import lax
from jax.experimental import pallas as pl
from jax.experimental.pallas import tpu as pltpu
from jax.sharding import PartitionSpec as P

KSIZE = 41
NBASIS = 16
NTERMS = 6
TOP = 2
BLK = 40
PATCH = 256
HALF = 20
BLKIN = 80
LANES = 128
WIDTH = 1664
EXTRA = 1600 % LANES

SIGMAS = (0.7, 1.5, 3.0, 2.0)
POWERS = (0, 0, 0, 1)
COLUMN_AT = (0, 40, 80, 128)


DEEP = 16
START = (2, 9)
FIRST = 5


def visit_order(count):
    wide = count // DEEP
    return [
        (x + START[0]) % wide * DEEP + (z + START[1]) % DEEP for x in range(wide) for z in range(DEEP)
    ]


def tract_order(count):
    return [(t + FIRST) % count for t in range(count)]


def constant_tables():
    difference = np.arange(BLKIN)[None, :] - np.arange(BLK)[:, None]
    inside = (difference >= 0) & (difference < KSIZE)
    shifted = (difference - HALF).astype(np.float32)
    taps = np.arange(KSIZE, dtype=np.float32) - np.float32(HALF)
    tables = []
    for sigma, power in zip(SIGMAS, POWERS):

        def profile(offset):
            value = np.exp(-offset * offset / np.float32(2.0 * sigma * sigma)).astype(np.float32)
            if power == 1:
                value = value * offset / np.float32(sigma)
            return value.astype(np.float32)

        total = np.sum(np.abs(profile(taps)), dtype=np.float32)
        tables.append(np.where(inside, profile(shifted) / total, np.float32(0.0)))
    held = np.zeros((4 * BLK + LANES, 2 * LANES), np.float32)
    held[: 4 * BLK, :BLKIN] = np.concatenate(tables, axis=0)
    for c, at in enumerate(COLUMN_AT):
        held[4 * BLK : 4 * BLK + BLKIN, at : at + BLK] = tables[c].T
    return jnp.asarray(held, jnp.bfloat16)


def warp_kernel(
    images_ref,
    coefficients_ref,
    orders_ref,
    resample_ref,
    weights_ref,
    routes_ref,
    offsets_ref,
    tables_ref,
    out_ref,
    image_rows,
    resample_rows,
    planes,
    warped_rows,
    flat,
    *held,
):
    f32, bf16 = jnp.float32, jnp.bfloat16
    *held, arrival = held
    sources = (
        images_ref,
        resample_ref,
        coefficients_ref,
        orders_ref,
        weights_ref,
        routes_ref,
        offsets_ref,
        tables_ref,
    )
    copies = [
        pltpu.make_async_copy(source, kept, arrival.at[number])
        for number, (source, kept) in enumerate(zip(sources, held, strict=True))
    ]
    for copy in copies:
        copy.start()
    (
        images_ref,
        resample_ref,
        coefficients_ref,
        orders_ref,
        weights_ref,
        routes_ref,
        offsets_ref,
        tables_ref,
    ) = held
    copies[0].wait()
    blocks = images_ref.shape[0]
    wide = 2 * LANES

    for x in range(BLKIN):
        start = min(x * BLKIN, BLKIN * BLKIN - LANES)
        piece = images_ref[:, start : start + LANES].astype(f32)
        if start != x * BLKIN:
            piece = jnp.roll(piece, start - x * BLKIN, axis=1)
        image_rows[pl.ds(x, blocks, stride=BLKIN + 1), :] = piece
    copies[1].wait()
    for copy in copies[2:]:
        copy.wait()
    for x in range(2 * BLK):
        start = min(x * BLK, 2 * BLK * BLK - LANES)
        piece = resample_ref[:, start : start + LANES].astype(f32)
        if start != x * BLK:
            piece = jnp.roll(piece, start - x * BLK, axis=1)
        resample_rows[pl.ds(x, blocks, stride=2 * BLK + 1), :] = piece

    terms = jnp.concatenate(
        [coefficients_ref[:, 4 * NTERMS * r : 4 * NTERMS * (r + 1)] for r in range(4)], axis=0
    )
    term_id = lax.broadcasted_iota(jnp.int32, (4 * NTERMS, wide), 0)
    lane = lax.broadcasted_iota(jnp.int32, (4 * NTERMS, wide), 1)
    column_kernel = sum((lane >= at).astype(jnp.int32) for at in COLUMN_AT[1:])
    spread = jnp.concatenate(
        [
            jnp.where(term_id == NTERMS * column_kernel + m, 1.0, 0.0).astype(bf16)
            for m in range(NTERMS)
        ],
        axis=1,
    )
    spread = jnp.dot(terms, spread, preferred_element_type=f32)
    lane = lax.broadcasted_iota(jnp.int32, (blocks, blocks), 1)
    sublane = lax.broadcasted_iota(jnp.int32, (blocks, blocks), 0)
    order = jnp.sum(
        jnp.where(lane == sublane, orders_ref[...].astype(f32), 0.0), axis=1, keepdims=True
    )
    order = jnp.concatenate([order] * 4, axis=0)
    first, second = order >= 1.0, order >= 2.0
    term = [spread[:, wide * m : wide * (m + 1)] for m in range(NTERMS)]
    term = (
        term[:1]
        + [jnp.where(first, t, 0.0) for t in term[1:3]]
        + [jnp.where(second, t, 0.0) for t in term[3:]]
    )
    lane = lax.broadcasted_iota(jnp.int32, (1, wide), 1)
    within = lane
    for at in COLUMN_AT[1:]:
        within = jnp.where(lane >= at, lane - at, within)
    across = (2.0 * within.astype(f32) + 1.0) / BLK - 1.0
    planes[:, :wide] = term[0] + across * (term[2] + across * term[5])
    planes[:, wide : 2 * wide] = term[1] + across * term[4]
    planes[:, 2 * wide :] = term[3]

    row_id = lax.broadcasted_iota(jnp.int32, (BLK, wide), 0).astype(f32)
    down = (2.0 * row_id + 1.0) / BLK - 1.0

    stacked = jnp.concatenate(
        [
            image_rows[(BLKIN + 1) * g : (BLKIN + 1) * g + BLKIN, :]
            for g in range(blocks)
        ],
        axis=1,
    ).astype(bf16)
    smooth = jnp.dot(tables_ref[: 4 * BLK, :BLKIN], stacked, preferred_element_type=f32).astype(bf16)
    responses = [
        jnp.dot(
            smooth[:, LANES * g : LANES * (g + 1)],
            tables_ref[4 * BLK :, :],
            preferred_element_type=f32,
        )
        for g in range(blocks)
    ]
    matched = []
    for g in range(blocks):
        total = jnp.zeros((BLK, wide), f32)
        for r in range(4):
            plane = planes[r * blocks + g : r * blocks + g + 1, :]
            weight = plane[:, :wide] + down * (
                plane[:, wide : 2 * wide] + down * plane[:, 2 * wide :]
            )
            total = total + weight * responses[g][BLK * r : BLK * (r + 1), :]
        low, high = total[:, :LANES], total[:, LANES:]
        folded = (
            low
            + high
            + pltpu.roll(low, LANES - BLK, axis=1)
            + pltpu.roll(low, LANES - 2 * BLK, axis=1)
        )
        matched.append(folded[:, :BLK].astype(bf16))
    halfway = [
        jnp.dot(
            resample_rows[(2 * BLK + 1) * g : (2 * BLK + 1) * g + BLK, :][:, :BLK].astype(bf16),
            matched[g],
            preferred_element_type=f32,
        ).astype(bf16)
        for g in range(blocks)
    ]
    warped = [
        lax.dot_general(
            halfway[g],
            resample_rows[(2 * BLK + 1) * g + BLK : (2 * BLK + 1) * (g + 1) - 1, :][:, :BLK].astype(bf16),
            (((1,), (1,)), ((), ())),
            preferred_element_type=f32,
        )
        for g in range(blocks)
    ]
    for g in range(blocks):
        warped_rows[(BLK + 1) * g : (BLK + 1) * g + BLK, 0:BLK] = warped[g]
    flat[:, 12 * LANES :] = jnp.zeros((blocks, LANES), f32)
    for i in range(BLK):
        flat[:, BLK * i : BLK * (i + 1)] = warped_rows[pl.ds(i, blocks, stride=BLK + 1), 0:BLK]
    pixels = flat[...].astype(bf16)

    slots, pairs = out_ref.shape[0] * out_ref.shape[1], TOP * blocks
    patch = jnp.concatenate([routes_ref[k : k + 1, :] for k in range(TOP)], axis=1)
    slot = lax.broadcasted_iota(jnp.int32, (slots, pairs), 0)
    place = slot // 2
    member = ((place + DEEP * START[0]) & (-DEEP & (slots // 2 - 1))) | (
        (place + START[1]) & (DEEP - 1)
    )
    hit = jnp.where(patch == member, 1.0, 0.0)
    before = lax.broadcasted_iota(jnp.int32, (pairs, pairs), 0)
    after = lax.broadcasted_iota(jnp.int32, (pairs, pairs), 1)
    rank = jnp.dot(
        hit.astype(bf16),
        jnp.where(before < after, 1.0, 0.0).astype(bf16),
        preferred_element_type=f32,
    )
    pick = jnp.where(rank == (slot % 2).astype(f32), hit, 0.0).astype(bf16)
    packed = jnp.dot(
        pick, jnp.concatenate([pixels] * TOP, axis=0), preferred_element_type=f32
    )
    column = lax.broadcasted_iota(jnp.int32, (LANES, pairs), 0) - EXTRA
    corner_y = jnp.concatenate([offsets_ref[k, 0:1, :] for k in range(TOP)], axis=1).astype(f32)
    corner_x = jnp.concatenate([offsets_ref[k, 1:2, :] for k in range(TOP)], axis=1).astype(f32)
    weight = jnp.concatenate([weights_ref[...].astype(f32)] * TOP, axis=1)
    extras = jnp.where(
        column == 0,
        corner_y,
        jnp.where(column == 1, corner_x, jnp.where(column == 2, weight, 0.0)),
    ).astype(bf16)
    tail = lax.dot_general(pick, extras, (((1,), (1,)), ((), ())), preferred_element_type=f32)
    packed = jnp.concatenate([packed[:, : 12 * LANES], packed[:, 12 * LANES :] + tail], axis=1)
    out_ref[...] = packed.astype(bf16).reshape(out_ref.shape)


def warp_and_pack(images, coefficients, orders, resample, weights, routes, offsets, slots):
    blocks = images.shape[0]
    f32 = jnp.float32
    operands = (
        images,
        coefficients,
        orders,
        resample,
        weights,
        jnp.transpose(routes, (1, 0)),
        jnp.transpose(offsets, (1, 2, 0)),
        constant_tables(),
    )
    kept = [operands[n] for n in (0, 3, 1, 2, 4, 5, 6, 7)]
    return pl.pallas_call(
        warp_kernel,
        out_shape=jax.ShapeDtypeStruct((slots // 2, 2, WIDTH), jnp.bfloat16),
        in_specs=[pl.BlockSpec(memory_space=pl.ANY)] * len(operands),
        scratch_shapes=[
            pltpu.VMEM(((blocks + 1) * (BLKIN + 1), LANES), f32),
            pltpu.VMEM(((blocks + 1) * (2 * BLK + 1), LANES), f32),
            pltpu.VMEM((blocks * 4, 3 * 2 * LANES), f32),
            pltpu.VMEM(((blocks + 1) * (BLK + 1), LANES), f32),
            pltpu.VMEM((blocks, WIDTH), f32),
            *[pltpu.VMEM(array.shape, array.dtype) for array in kept],
            pltpu.SemaphoreType.DMA((len(kept),)),
        ],
        compiler_params=pltpu.CompilerParams(vmem_limit_bytes=32 << 20),
        name="warp_and_pack",
    )(*[pltpu.with_memory_space_constraint(array, pltpu.HBM) for array in operands])


def place_kernel(parcel_ref, out_ref, slot_rows, spread_left, spread_right, corner_x_wide, row_hits):
    f32, bf16 = jnp.float32, jnp.bfloat16
    slots = parcel_ref.shape[0]
    tracts, rows = out_ref.shape[0], PATCH // out_ref.shape[0]
    pitch = slots + 1

    for i in range(BLK):
        start = min(i * BLK, WIDTH - LANES)
        piece = parcel_ref[:, start : start + LANES].astype(f32)
        if start != i * BLK:
            piece = jnp.roll(piece, start - i * BLK, axis=1)
        slot_rows[pl.ds(i, slots, stride=BLK + 1), :] = piece
    tail = parcel_ref[:, WIDTH - LANES :].astype(f32)
    corner_x = tail[:, EXTRA + 1 : EXTRA + 2]
    corner_x_wide[...] = jnp.broadcast_to(corner_x, (slots, PATCH))
    by_slot = jnp.transpose(tail, (1, 0))
    corner_y = by_slot[EXTRA : EXTRA + 1, :]
    corner_x_row = by_slot[EXTRA + 1 : EXTRA + 2, :]
    weight = by_slot[EXTRA + 2 : EXTRA + 3, :]

    shift = (
        lax.broadcasted_iota(jnp.int32, (BLK, PATCH), 1)
        - lax.broadcasted_iota(jnp.int32, (BLK, PATCH), 0)
    ).astype(f32)
    batch = 16
    for first in range(0, slots, batch):
        placed = []
        for s in range(first, first + batch):
            column = jnp.where(shift == corner_x_wide[s : s + 1, :], 1.0, 0.0).astype(bf16)
            block = slot_rows[(BLK + 1) * s : (BLK + 1) * s + BLK, :][:, :BLK].astype(bf16)
            placed.append(jnp.dot(block, column, preferred_element_type=f32))
        for s in range(first, first + batch):
            spread_left[pl.ds(s, BLK, stride=pitch), :] = placed[s - first][:, :LANES]
            spread_right[pl.ds(s, BLK, stride=pitch), :] = placed[s - first][:, LANES:]

    shifted = lax.broadcasted_iota(jnp.int32, (PATCH + BLK, slots), 0).astype(f32) - corner_y
    row_hits[...] = jnp.where(shifted == float(BLK), weight, 0.0)
    flux = jnp.zeros((PATCH, PATCH), f32)
    depth = 2
    for i in range(0, BLK, depth):
        row = jnp.concatenate(
            [row_hits[BLK - i - n : BLK - i - n + PATCH, :].astype(bf16) for n in range(depth)], axis=1
        )
        across = jnp.concatenate(
            [
                jnp.concatenate(
                    [half[pitch * (i + n) : pitch * (i + n) + slots, :] for n in range(depth)], axis=0
                )
                for half in (spread_left, spread_right)
            ],
            axis=1,
        ).astype(bf16)
        flux += jnp.dot(row, across, preferred_element_type=f32)
    blank = jnp.zeros((6, PATCH), f32)
    for place, t in enumerate(tract_order(tracts)):
        corners = jnp.concatenate([corner_y - float(rows * t), corner_x_row], axis=1)
        weights = jnp.concatenate([weight, jnp.zeros_like(weight)], axis=1)
        parts = [flux[rows * t : rows * (t + 1), :], corners, weights, blank]
        out_ref[place] = jnp.concatenate(parts, axis=0).astype(bf16)


def place(parcel, tracts):
    slots = parcel.shape[0]
    f32 = jnp.float32
    return pl.pallas_call(
        place_kernel,
        out_shape=jax.ShapeDtypeStruct((tracts, PATCH // tracts + 8, PATCH), jnp.bfloat16),
        scratch_shapes=[
            pltpu.VMEM(((slots + 1) * (BLK + 1), LANES), f32),
            pltpu.VMEM(((slots + 1) * (BLK + 1), LANES), f32),
            pltpu.VMEM(((slots + 1) * (BLK + 1), LANES), f32),
            pltpu.VMEM((slots, PATCH), f32),
            pltpu.VMEM((PATCH + BLK, slots), f32),
        ],
        compiler_params=pltpu.CompilerParams(vmem_limit_bytes=24 << 20),
        name="place_in_patch",
    )(parcel)


def finish_kernel(parts_ref, flux_ref, cover_ref):
    f32, bf16 = jnp.float32, jnp.bfloat16
    rows, slots = flux_ref.shape[0], PATCH // 2
    y = lax.broadcasted_iota(jnp.int32, (rows, slots), 0).astype(f32)
    x = lax.broadcasted_iota(jnp.int32, (PATCH, slots), 0).astype(f32)
    flux = jnp.zeros((rows, PATCH), f32)
    cover = jnp.zeros((rows, PATCH), f32)
    for t in range(parts_ref.shape[0]):
        part = parts_ref[t].astype(f32)
        flux += part[:rows, :]
        extras = part[rows:, :]
        down = y - extras[0:1, :slots]
        across = x - extras[0:1, slots:]
        row = jnp.where((down >= 0.0) & (down < float(BLK)), extras[1:2, :slots], 0.0)
        column = jnp.where((across >= 0.0) & (across < float(BLK)), 1.0, 0.0)
        cover += lax.dot_general(
            row.astype(bf16),
            column.astype(bf16),
            (((1,), (1,)), ((), ())),
            preferred_element_type=f32,
        )
    flux_ref[...] = flux
    cover_ref[...] = cover


def finish(parts, tracts):
    out = jax.ShapeDtypeStruct((PATCH // tracts, PATCH), jnp.float32)
    return pl.pallas_call(
        finish_kernel,
        out_shape=(out, out),
        compiler_params=pltpu.CompilerParams(vmem_limit_bytes=16 << 20),
        name="finish",
    )(parts)


def per_device(images, coefficients, orders, resample, weights, routes, offsets):
    visit_count = lax.axis_size("visit")
    tract_count = lax.axis_size("tract")
    capacity = 2
    slot_count = visit_count * capacity
    parcel = warp_and_pack(
        images[0],
        coefficients[0],
        orders,
        resample[0],
        weights,
        routes[0],
        offsets[0],
        slot_count,
    )
    parcel = lax.all_to_all(
        parcel,
        "visit",
        split_axis=0,
        concat_axis=0,
        tiled=True,
        axis_index_groups=[visit_order(visit_count)],
    ).reshape(slot_count, WIDTH)
    parts = place(parcel, tract_count)
    parts = lax.all_to_all(
        parts,
        "tract",
        split_axis=0,
        concat_axis=0,
        tiled=True,
        axis_index_groups=[tract_order(tract_count)],
    )
    flux, cover = finish(parts, tract_count)
    return (flux[None], cover[None])


def solution(mesh):
    in_specs = (
        P("tract", "visit", None),
        P("tract", "visit", None),
        P("tract", "visit"),
        P("tract", "visit", None),
        P("tract", "visit"),
        P("tract", "visit", None),
        P("tract", "visit", None, None),
    )
    out_specs = (P("visit", "tract", None), P("visit", "tract", None))
    return jax.shard_map(
        per_device, mesh=mesh, in_specs=in_specs, out_specs=out_specs, check_vma=False
    )
```
